32 devices in a mesh: groups: 2 (over y), rows: 4 (over z), cols: 2 (over x), rhs: 2 (over core).
Axes of the slice: x: 2, y: 2, z: 4, core: 2. Of those that a mesh axis runs over, the one named last changes fastest.
Arguments:
- influence: bfloat16 [32768, 16384], P(('groups', 'rows'), 'cols'), parts along dimension 0, may hold values from -0.046875 to 0.046875
- wake_influence: bfloat16 [32768, 1024], P(('groups', 'rows'), 'cols'), parts along dimension 0, may hold values from -0.0234375 to 0.0234375
- self_term: float32 [32768], P(('groups', 'rows')), parts along dimension 0, may hold values from 2 to 4
- wake_upper: int32 [2048], P(('groups', 'cols')), parts along dimension 0, may hold values from 0 to 16383, as said below
- wake_lower: int32 [2048], P(('groups', 'cols')), parts along dimension 0, may hold values from 0 to 16383, as said below
- blade_of: int32 [32768], P(('groups', 'rows')), parts along dimension 0, may hold values from 0 to 4, never falling along the last dimension, each value on 1 to 4096 neighbouring positions
- mode_shapes: float32 [16, 16384], P(None, 'rows'), may hold values from -100 to 100
- blade_pitch: float32 [5, 16], P(None, 'rhs'), may hold values from 0.5 to 2
- design_map: int32 [16], P('rhs'), may hold values from 0 to 15
- objectives: float32 [16, 16384], P('rhs', 'rows'), may hold values from -6 to 6
Outputs:
- solution: float32 [16, 32768], P('rhs', ('groups', 'rows', 'cols')), parts along dimension 1
- adjoint: float32 [16, 32768], P('rhs', ('groups', 'rows', 'cols')), parts along dimension 1
The draws below stay inside these ranges and needn't reach their ends.
There are 2 independent parts, one for each index of `groups`. The reference program is written for one: setup_inputs(seed, part) draws one part's arguments, and reference() takes and returns one part's arrays. A program takes and returns all parts, laid end to end along the dimension named above; an argument that names none is the same for every part. Nothing has to cross between parts.
Inputs may be any that keep to these rules, and one draw needn't show every extreme that they name: `wake_upper`: the two trailing-edge panels of wake panel j differ and both lie among panels c * 8192 to (c + 1) * 8192 - 1, where c = j // 512. `wake_lower`: the two trailing-edge panels of wake panel j differ and both lie among panels c * 8192 to (c + 1) * 8192 - 1, where c = j // 512.
All inputs are finite; a program needn't handle non-finite values.
Results may differ from the reference program's by a relative error of at most 0.0013.
Values may be sent and summed in bfloat16 or wider, within the bound.
No kernel may reach another device: no remote copies, remote signals or barrier semaphores. Data moves between devices by JAX's collectives and lax.ppermute only.
A program may use at most 192 MiB of HBM per device.

```python
import math
import jax
import jax.numpy as jnp
import numpy as np
from jax import lax

PANELS = 16384
WAKE = 1024
BLOCK = 8
RHS_BLOCKS = 2
DESIGN = 16
BLADES = 5
ITERS = 2
ADJOINT_STEPS = 2
RHS = 16
OBJECTIVES = 16
COL_PANELS = 8192
WAKE_COL = 512


def wake_pair(key):
    first_key = jax.random.fold_in(key, 11)
    second_key = jax.random.fold_in(key, 12)
    block_start = jnp.arange(WAKE, dtype=jnp.int32) // WAKE_COL * COL_PANELS
    upper_local = jax.random.randint(first_key, (WAKE,), 0, COL_PANELS, dtype=jnp.int32)
    offset = jax.random.randint(second_key, (WAKE,), 1, COL_PANELS, dtype=jnp.int32)
    return (block_start + upper_local, block_start + (upper_local + offset) % COL_PANELS)


def draw_wake_upper(key, part):
    return wake_pair(key)[0]


def draw_wake_lower(key, part):
    return wake_pair(key)[1]


def draw_mode_shapes(key, part):
    keys = jax.random.split(key, 3)
    position = jnp.arange(PANELS, dtype=jnp.float32) / PANELS
    row_scale = jnp.exp(jax.random.uniform(keys[1], (1, PANELS)) * math.log(10.0))
    row_scale = row_scale * jnp.exp(position * math.log(3.0))[None, :]
    col_scale = jnp.exp(jax.random.uniform(keys[2], (DESIGN, 1)) * math.log(10.0))
    base = jnp.clip(jax.random.normal(keys[0], (DESIGN, PANELS)), -4.0, 4.0)
    return jnp.clip(base * row_scale * col_scale / 15.0, -100.0, 100.0)


def place_ends(array, key, least, top_value):
    index_at = [jax.random.randint(jax.random.fold_in(key, axis), (), 0, length) for axis, length in enumerate(array.shape)]
    widest = array.shape.index(max(array.shape))
    neighbour = index_at[:widest] + [(index_at[widest] + 1) % array.shape[widest]] + index_at[widest + 1:]
    return array.at[tuple(index_at)].set(least).at[tuple(neighbour)].set(top_value)


def block_levels(key, shape, cuts, low, top_value):
    gain, own = 1.0, jax.random.fold_in(key, 6)
    for axis_at, blocks in cuts:
        steps = jnp.exp(jax.random.uniform(jax.random.fold_in(own, axis_at), (blocks,), jnp.float32, low / len(cuts), top_value / len(cuts)))
        gain = gain * jnp.repeat(steps, shape[axis_at] // blocks).reshape([-1 if axis == axis_at else 1 for axis in range(len(shape))])
    return gain


def split_up(amount, total, reach, slope):
    portions = [(1 << 20) // math.isqrt(grade ** slope) + 1 for grade in range(2, amount + 1)]
    spare, counts = total - reach - (amount - 1), [1] * (amount - 1)
    while spare > 0:
        candidates = [i for i in range(amount - 1) if counts[i] < reach]
        mass, left = sum([portions[i] for i in candidates]), spare
        for i in candidates:
            more = min(reach - counts[i], max(1, left * portions[i] // mass), spare)
            counts[i] = counts[i] + more
            spare = spare - more
    return np.array([reach] + counts)


def ragged_sizes(own_key, number_of, total, reach, lean):
    if number_of == 2:
        one = jax.random.randint(own_key, (), max(1, total - reach), min(reach, total - 1) + 1)
        return jnp.stack([one, total - one])
    sizes = jnp.asarray(split_up(number_of, total, reach, lean), jnp.int32)
    couples = (number_of - 1) // 2
    giver, taker = sizes[1:1 + 2 * couples:2], sizes[2:2 + 2 * couples:2]
    room = jnp.minimum(giver - 1, reach - taker)
    shifted = jax.random.randint(jax.random.fold_in(own_key, 1), (couples,), 0, 1 << 20) % (room + 1)
    sizes = sizes.at[1:1 + 2 * couples:2].set(giver - shifted).at[2:2 + 2 * couples:2].set(taker + shifted)
    return sizes[jax.random.permutation(jax.random.fold_in(own_key, 2), number_of)]


def bell_draw(key, extent, deviation, bound, pieces=(), kind=jnp.bfloat16):
    values = deviation * jax.random.normal(key, extent, jnp.float32)
    if pieces:
        values = values * block_levels(key, extent, pieces, -0.22, 0.18)
    return jnp.clip(values, -bound, bound).astype(kind)


def setup_inputs(seed: int = 0, part: int = 0) -> dict:
    streams_of = jax.random.split(jax.random.key(seed), 11)
    own_keys = jax.random.split(jax.random.fold_in(streams_of[10], part), 11)
    influence = bell_draw(own_keys[0], (PANELS, PANELS), PANELS ** -0.5, 0.046875, ((0, 4), (1, 2)))
    wake_influence = bell_draw(own_keys[1], (PANELS, WAKE), (64 * WAKE) ** -0.5, 0.0234375, ((0, 4), (1, 2)))
    self_term = jnp.clip(2.0 + 2.0 * jax.random.uniform(own_keys[2], (PANELS,), jnp.float32) ** block_levels(own_keys[2], (PANELS,), ((0, 4),), -0.2, 0.2), 2.0, 4.0)
    wake_upper = draw_wake_upper(jax.random.fold_in(jax.random.fold_in(streams_of[10], part), 71), part)
    wake_lower = draw_wake_lower(jax.random.fold_in(jax.random.fold_in(streams_of[10], part), 71), part)
    blade_of = jnp.searchsorted(jnp.cumsum(ragged_sizes(own_keys[5], BLADES, PANELS, PANELS // 4, 0)), jnp.arange(PANELS), side="right").astype(jnp.int32)
    mode_shapes = draw_mode_shapes(jax.random.fold_in(streams_of[10], 71), part)
    blade_pitch = jnp.clip(jnp.exp(math.log(2.0) - 1.3862944 * jax.random.uniform(streams_of[7], (BLADES, RHS), jnp.float32) ** block_levels(streams_of[7], (BLADES, RHS), ((1, 2),), -0.2, 0.2)), 0.5, 2.0)
    design_map = place_ends(jax.random.randint(streams_of[8], (RHS,), 0, DESIGN), jax.random.fold_in(streams_of[8], 1), 0, DESIGN - 1).astype(jnp.int32)
    objectives = bell_draw(streams_of[9], (OBJECTIVES, PANELS), 1.0, 6.0, ((0, 2), (1, 4)), jnp.float32)
    return {"influence": influence, "wake_influence": wake_influence, "self_term": self_term, "wake_upper": wake_upper, "wake_lower": wake_lower, "blade_of": blade_of, "mode_shapes": mode_shapes, "blade_pitch": blade_pitch, "design_map": design_map, "objectives": objectives}


def product(left, right, dims):
    return lax.dot_general(left.astype(jnp.float32), right.astype(jnp.float32), (dims, ((), ())), preferred_element_type=jnp.float32)

def precise(left, right, dims):
    return lax.dot_general(left, right, (dims, ((), ())), precision=lax.Precision.HIGHEST)

def forward(field, influence, wake_influence, self_term, wake_upper, wake_lower):
    rounded = field.astype(jnp.bfloat16)
    values = rounded.astype(jnp.float32)
    strength = (values[:, wake_upper] - values[:, wake_lower]).astype(jnp.bfloat16)
    image = product(rounded, influence, ((1,), (1,)))
    image = image + product(strength, wake_influence, ((1,), (1,)))
    return image + self_term[None, :] * field

def block_gmres(right_block, influence, wake_influence, self_term, wake_upper, wake_lower):
    lower_start = jnp.linalg.cholesky(precise(right_block, right_block, ((1,), (1,))))
    bases = [jax.scipy.linalg.solve_triangular(lower_start, right_block, lower=True)]
    columns = []
    for step in range(ITERS):
        image = forward(bases[-1], influence, wake_influence, self_term, wake_upper, wake_lower)
        stacked = jnp.concatenate(bases, axis=0)
        coeffs = precise(stacked, image, ((1,), (1,)))
        image = image - precise(coeffs, stacked, ((0,), (0,)))
        factor = jnp.linalg.cholesky(precise(image, image, ((1,), (1,))))
        if step + 1 < ITERS:
            bases.append(jax.scipy.linalg.solve_triangular(factor, image, lower=True))
        padding = jnp.zeros((BLOCK * (ITERS - 1 - step), BLOCK), jnp.float32)
        columns.append(jnp.concatenate([coeffs, factor.T, padding], axis=0))
    hessen = jnp.concatenate(columns, axis=1)
    target = jnp.concatenate([lower_start.T, jnp.zeros((BLOCK * ITERS, BLOCK), jnp.float32)], axis=0)
    normal_matrix = precise(hessen, hessen, ((0,), (0,)))
    right_term = precise(hessen, target, ((0,), (0,)))
    weights = jax.scipy.linalg.cho_solve((jnp.linalg.cholesky(normal_matrix), True), right_term)
    return precise(weights, jnp.concatenate(bases, axis=0), ((0,), (0,)))

def reference(influence, wake_influence, self_term, wake_upper, wake_lower, blade_of, mode_shapes, blade_pitch, design_map, objectives):
    mode_picks = mode_shapes[design_map]
    blade_factor = blade_pitch[blade_of].T
    right_side = mode_picks * blade_factor
    blocks = []
    for number in range(RHS_BLOCKS):
        right_block = right_side[number * BLOCK:(number + 1) * BLOCK]
        blocks.append(block_gmres(right_block, influence, wake_influence, self_term, wake_upper, wake_lower))
    solution = jnp.concatenate(blocks, axis=0)
    adjoint = objectives / self_term[None, :]
    for step in range(ADJOINT_STEPS):
        rounded = adjoint.astype(jnp.bfloat16)
        carried = product(rounded, wake_influence, ((1,), (0,)))
        spread = jnp.zeros((OBJECTIVES, PANELS), jnp.float32)
        spread = spread.at[:, wake_upper].add(carried).at[:, wake_lower].add(-carried)
        image = product(rounded, influence, ((1,), (0,))) + spread + self_term[None, :] * adjoint
        adjoint = adjoint + (objectives - image) / self_term[None, :]
    return (solution, adjoint)
```

```python
import functools

import jax
import jax.numpy as jnp
from jax import lax
from jax.experimental import pallas as pl
from jax.experimental.pallas import tpu as pltpu
from jax.sharding import PartitionSpec as P

BLOCK = 8
LANES = 128
SHIFT = 3.0
GRID = ("rows", "cols", "rhs")
PLANE = ("cols", "rhs")
F32 = jnp.float32
BF16 = jnp.bfloat16

VMEM = pl.BlockSpec(memory_space=pltpu.VMEM)
SMEM = pl.BlockSpec(memory_space=pltpu.SMEM)
ANY = pl.BlockSpec(memory_space=pl.ANY)


def dot(left, right, dims):
    return lax.dot_general(left, right, (dims, ((), ())), preferred_element_type=F32)


def precise(left, right, dims):
    return lax.dot_general(
        left, right, (dims, ((), ())), precision=lax.Precision.HIGHEST, preferred_element_type=F32
    )


def low_onehot(index):
    low = jnp.bitwise_and(index, LANES - 1)
    hit = lax.broadcasted_iota(jnp.int32, (LANES, index.shape[1]), 0) == low
    return jnp.where(hit, 1.0, 0.0).astype(BF16)


def take_columns(field, index):
    rows, width = field.shape
    chunks = width // LANES
    stacked = jnp.concatenate(
        [field[:, i * LANES : (i + 1) * LANES] for i in range(chunks)], axis=0
    )
    picked = dot(stacked, low_onehot(index), ((1,), (0,)))
    high = jnp.right_shift(index, 7)
    total = jnp.zeros((rows, index.shape[1]), F32)
    for i in range(chunks):
        total = total + jnp.where(high == i, picked[i * rows : (i + 1) * rows], 0.0)
    return total


def put_columns(values, index, width):
    rows = values.shape[0]
    chunks = width // LANES
    upper = values.astype(BF16).astype(F32)
    parts = (upper, values - upper)
    high = jnp.right_shift(index, 7)
    onehot = low_onehot(index)
    total = None
    for part in parts:
        stacked = jnp.concatenate(
            [jnp.where(high == i, part, 0.0).astype(BF16) for i in range(chunks)], axis=0
        )
        spread = dot(stacked, onehot, ((1,), (1,)))
        total = spread if total is None else total + spread
    return jnp.concatenate([total[i * rows : (i + 1) * rows] for i in range(chunks)], axis=1)


def gather_shards(scalars, shards, out, shard, slot):
    if len(shards) == 1:
        out[:, 0 : shards[0].shape[1]] = shards[0][...]
        return
    for k, ref in enumerate(shards):
        start = pl.multiple_of(jnp.bitwise_xor(scalars[slot], k) * shard, LANES)
        out[:, pl.ds(start, shard)] = ref[...]


def emit_shards(scalars, whole, outs, shard, slot):
    if len(outs) == 1:
        outs[0][...] = whole[:, 0 : outs[0].shape[1]]
        return
    for k, ref in enumerate(outs):
        start = pl.multiple_of(jnp.bitwise_xor(scalars[slot], k) * shard, LANES)
        ref[...] = whole[:, pl.ds(start, shard)]


def finish_adjoint(scalars, upper, lower, whole, outs, piece, shard):
    carried = whole[:, piece:]
    whole[:, 0:piece] += put_columns(carried, upper[...], piece) - put_columns(
        carried, lower[...], piece
    )
    emit_shards(scalars, whole, outs, shard, 0)


def load_adjoint_kernel(
    chunk, n_out, shard, scalars, field, upper, lower, influence, wake, *rest
):
    outs, (held, whole, sems) = rest[:n_out], rest[n_out:]
    piece = held.shape[1] - wake.shape[1]
    rows = held.shape[0]
    steps = rows // chunk
    first = pl.multiple_of(scalars[2] * piece, LANES)

    def copies(i):
        span = pl.ds(i * chunk, chunk)
        return (
            pltpu.make_async_copy(
                influence.at[span, pl.ds(first, piece)],
                held.at[span, pl.ds(0, piece)],
                sems.at[0, i],
            ),
            pltpu.make_async_copy(
                wake.at[span], held.at[span, pl.ds(piece, wake.shape[1])], sems.at[1, i]
            ),
        )

    for i in range(steps):
        for copy in copies(i):
            copy.start()
    for i in range(steps):
        for copy in copies(i):
            copy.wait()
        span = slice(i * chunk, (i + 1) * chunk)
        part = dot(field[:, span], held[span, :], ((1,), (0,)))
        if i == 0:
            whole[...] = part
        else:
            whole[...] += part
    finish_adjoint(scalars, upper, lower, whole, outs, piece, shard)


def adjoint_kernel(tile, n_in, n_out, shard, scalars, upper, lower, held, *rest):
    shards, outs, (field, whole) = rest[:n_in], rest[n_in : n_in + n_out], rest[n_in + n_out :]
    gather_shards(scalars, shards, field, shard, 1)
    width = held.shape[1]
    for start in range(0, width, tile):
        stop = min(width, start + tile)
        whole[:, start:stop] = dot(field[...], held[:, start:stop], ((1,), (0,)))
    piece = width - upper.shape[1]
    finish_adjoint(scalars, upper, lower, whole, outs, piece, shard)


def forward_kernel(tile, n_in, n_out, shard, scalars, upper, lower, held, *rest):
    shards, outs, (field, whole) = rest[:n_in], rest[n_in : n_in + n_out], rest[n_in + n_out :]
    piece = held.shape[1] - upper.shape[1]
    gather_shards(scalars, shards, field, shard, 0)
    source = field[:, 0:piece]
    strength = take_columns(source, upper[...]) - take_columns(source, lower[...])
    field[:, piece:] = strength.astype(BF16)
    for start in range(0, held.shape[0], tile):
        whole[:, start : start + tile] = dot(
            field[...], held[start : start + tile, :], ((1,), (1,))
        )
    emit_shards(scalars, whole, outs, shard, 1)


def inverse_factor(gram):
    size = gram.shape[0]
    row = lax.broadcasted_iota(jnp.int32, (size, size), 0)
    col = lax.broadcasted_iota(jnp.int32, (size, size), 1)
    left = jnp.where(row == col, 1.0, 0.0)
    for j in range(size - 1):
        scale = jnp.where(
            row[:, 0:1] > j, gram[:, j : j + 1] / gram[j : j + 1, j : j + 1], 0.0
        )
        left = left - scale * left[j : j + 1, :]
        gram = gram - scale * gram[j : j + 1, :]
    pivots = jnp.sum(jnp.where(row == col, gram, 0.0), axis=1, keepdims=True)
    return left / jnp.sqrt(pivots)


def start_kernel(n_parts, right_piece, right_shard, *rest):
    parts, (rounded, basis) = rest[:n_parts], rest[n_parts:]
    gram = parts[0][...]
    for part in parts[1:]:
        gram = gram + part[...]
    for b in range(gram.shape[0] // BLOCK):
        span = slice(b * BLOCK, (b + 1) * BLOCK)
        inverse = inverse_factor(gram[span, span])
        rounded[span, :] = precise(inverse, right_piece[span, :], ((1,), (0,))).astype(BF16)
        basis[span, :] = precise(inverse, right_shard[span, :], ((1,), (0,)))


def solve_kernel(parts, basis, out):
    system = jnp.sum(parts[...], axis=0)
    size = basis.shape[0]
    row = lax.broadcasted_iota(jnp.int32, (size, 1), 0)
    for j in range(size):
        pivot_row = system[j : j + 1, :] / system[j : j + 1, j : j + 1]
        factor = jnp.where(row == j, 0.0, system[:, j : j + 1])
        system = jnp.where(row == j, pivot_row, system - factor * pivot_row)
    weights = system[:, size : size + BLOCK]
    out[...] = precise(weights, basis[...], ((0,), (0,)))


def params(mib):
    return pltpu.CompilerParams(vmem_limit_bytes=mib << 20)


def per_device(
    influence,
    wake_influence,
    self_term,
    wake_upper,
    wake_lower,
    blade_of,
    mode_shapes,
    blade_pitch,
    design_map,
    objectives,
):
    n_rows, n_cols, n_rhs = (lax.axis_size(name) for name in GRID)
    side = n_cols * n_rhs
    row_panels, col_panels = influence.shape
    wake = wake_influence.shape[1]
    piece = col_panels // n_rhs
    shard = row_panels // side
    count = 2 * BLOCK
    if n_rows != side or n_rhs != 2 or piece != row_panels:
        raise ValueError("unsupported mesh")
    aligned = shard % LANES == 0
    row_index = lax.axis_index("rows")
    core = lax.axis_index("rhs")
    plane_index = lax.axis_index("cols") * n_rhs + core

    def cross(k):
        return [(a * side + b, (b ^ k) * side + a) for a in range(side) for b in range(side)]

    def cross_back(k):
        return [(a * side + b, b * side + (a ^ k)) for a in range(side) for b in range(side)]

    def flip(k, size):
        return [(i, i ^ k) for i in range(size)]

    def swap(value):
        return lax.ppermute(value, "rhs", flip(1, 2))

    def both(own, other, axis):
        first = jnp.where(core == 0, own, other)
        second = jnp.where(core == 0, other, own)
        return jnp.concatenate([first, second], axis=axis)

    def pick(value, k_slot, k):
        return lax.dynamic_slice_in_dim(value, jnp.bitwise_xor(k_slot, k) * shard, shard, 1)

    def split(arrays, slot):
        return arrays if aligned else [pick(arrays[0], slot, k) for k in range(side)]

    def join(shards, slot):
        if aligned:
            return shards
        out = jnp.zeros((count, shard * side), shards[0].dtype)
        for k, value in enumerate(shards):
            out = lax.dynamic_update_slice_in_dim(
                out, value, jnp.bitwise_xor(slot, k) * shard, 1
            )
        return [out]

    n_out = side if aligned else 1
    out_width = shard if aligned else piece
    shard_shapes = [jax.ShapeDtypeStruct((count, out_width), F32)] * n_out

    scalars = jnp.stack([row_index, plane_index, core]).astype(jnp.int32)
    local_upper = (wake_upper - plane_index * piece)[None, :]
    local_lower = (wake_lower - plane_index * piece)[None, :]

    small = jnp.concatenate([blade_pitch, design_map[None, :].astype(F32)], axis=0)
    small = both(small, swap(small), 1)
    pitch = small[:-1]
    modes = small[-1].astype(jnp.int32)
    targets = both(objectives, swap(objectives), 0)

    mode_onehot = (
        modes[:, None] == jnp.arange(mode_shapes.shape[0], dtype=jnp.int32)[None, :]
    ).astype(F32)
    mode_picks = jnp.sum(mode_onehot[:, :, None] * mode_shapes[None, :, :], axis=1)
    blade_onehot = (
        jnp.arange(pitch.shape[0], dtype=jnp.int32)[:, None] == blade_of[None, :]
    ).astype(F32)
    right = mode_picks * jnp.sum(pitch[:, :, None] * blade_onehot[:, None, :], axis=0)
    gram = precise(right, right, ((1,), (1,)))
    grams = [gram] + [lax.ppermute(gram, "rows", flip(k, n_rows)) for k in range(1, n_rows)]
    right_piece = lax.ppermute(right, GRID, cross(0))

    own = plane_index * shard
    self_shard = lax.dynamic_slice_in_dim(self_term, own, shard, 0)[None, :]
    target_shard = lax.dynamic_slice_in_dim(targets, own, shard, 1)
    right_shard = lax.dynamic_slice_in_dim(right, own, shard, 1)

    rounded = (targets / self_term[None, :]).astype(BF16)
    chunk = row_panels // 8
    width = piece + wake
    results = pl.pallas_call(
        functools.partial(load_adjoint_kernel, chunk, n_out, shard),
        in_specs=[SMEM, VMEM, VMEM, VMEM, ANY, ANY],
        out_specs=[VMEM] * (n_out + 1),
        out_shape=shard_shapes + [pltpu.VMEM((row_panels, width), BF16)],
        scratch_shapes=[
            pltpu.VMEM((count, width), F32),
            pltpu.SemaphoreType.DMA((2, row_panels // chunk)),
        ],
        compiler_params=params(16),
        name="load_adjoint",
    )(scalars, rounded, local_upper, local_lower, influence, wake_influence)
    held = results[-1]
    partial_images = split(results[:-1], row_index)

    def product(kernel, shards, held, name):
        held = pltpu.with_memory_space_constraint(held, pltpu.VMEM)
        field_width = width if kernel is forward_kernel else row_panels
        whole_width = row_panels if kernel is forward_kernel else width
        return pl.pallas_call(
            functools.partial(kernel, 512, len(shards), n_out, shard),
            in_specs=[SMEM] + [VMEM] * (3 + len(shards)),
            out_specs=[VMEM] * n_out,
            out_shape=shard_shapes,
            scratch_shapes=[
                pltpu.VMEM((count, field_width), BF16),
                pltpu.VMEM((count, whole_width), F32),
            ],
            compiler_params=params(16),
            cost_estimate=pl.CostEstimate(
                flops=2 * count * row_panels * width,
                bytes_accessed=2 * row_panels * width,
                transcendentals=0,
            ),
            name=name,
        )(scalars, local_upper, local_lower, held, *shards)

    def adjoint_update(previous, partials):
        image = self_shard * previous
        for k, value in enumerate(partials):
            image = image + lax.ppermute(value, GRID, cross_back(k))
        return previous + (target_shard - image) / self_shard

    def plane_sum(values):
        total = values[0]
        for k in range(1, side):
            total = total + lax.ppermute(values[k], PLANE, flip(k, side))
        return total

    start_rounded, basis = pl.pallas_call(
        functools.partial(start_kernel, len(grams)),
        in_specs=[VMEM] * (2 + len(grams)),
        out_specs=[VMEM, VMEM],
        out_shape=[
            jax.ShapeDtypeStruct((count, piece), BF16),
            jax.ShapeDtypeStruct((count, shard), F32),
        ],
        compiler_params=params(16),
        name="start",
    )(right_piece, right_shard, *grams)
    induced = split(product(forward_kernel, [start_rounded], held, "forward_one"), plane_index)
    adjoint = adjoint_update(target_shard / self_shard, partial_images)
    adjoint_rounded = adjoint.astype(BF16)
    adjoint_shards = [adjoint_rounded] + [
        lax.ppermute(adjoint_rounded, PLANE, flip(k, side)) for k in range(1, side)
    ]
    partial_images = split(
        product(adjoint_kernel, join(adjoint_shards, plane_index), held, "adjoint_two"), row_index
    )

    image = plane_sum(induced) + (self_shard - SHIFT) * basis
    image_rounded = image.astype(BF16)
    image_shards = [lax.ppermute(image_rounded, GRID, cross(k)) for k in range(side)]
    induced = split(
        product(forward_kernel, join(image_shards, row_index), held, "forward_two"), plane_index
    )
    first_image = image + SHIFT * basis
    second_image = plane_sum(induced) + self_shard * image

    images = jnp.concatenate([first_image, second_image], axis=0)
    system = precise(images, jnp.concatenate([images, right_shard], axis=0), ((1,), (1,)))
    system = system.reshape(2, 2, BLOCK, 3, 2, BLOCK)
    packs = [
        jnp.pad(
            system[:, b, :, :, b].reshape(count, 3 * BLOCK), ((0, 0), (0, LANES - 3 * BLOCK))
        )
        for b in range(2)
    ]
    packs = jnp.stack(packs * (side * n_rows // 2))
    packs = lax.all_to_all(packs, GRID, 0, 0, tiled=True)

    def own_rows(value):
        return lax.dynamic_slice_in_dim(value, core * BLOCK, BLOCK, 0)

    def other_rows(value):
        return lax.dynamic_slice_in_dim(value, (1 - core) * BLOCK, BLOCK, 0)

    def to_output(own_part, other_part):
        return both(own_part, swap(other_part), 1)

    bases = to_output(
        jnp.concatenate([own_rows(basis), own_rows(image)], axis=0),
        jnp.concatenate([other_rows(basis), other_rows(image)], axis=0),
    )
    solution = pl.pallas_call(
        solve_kernel,
        in_specs=[VMEM, VMEM],
        out_specs=VMEM,
        out_shape=jax.ShapeDtypeStruct((BLOCK, bases.shape[1]), F32),
        compiler_params=params(16),
        name="solve",
    )(packs, bases)
    adjoint = adjoint_update(adjoint, partial_images)
    adjoint = to_output(own_rows(adjoint), other_rows(adjoint))
    return (solution, adjoint)


def solution(mesh):
    in_specs = (
        P(("groups", "rows"), "cols"),
        P(("groups", "rows"), "cols"),
        P(("groups", "rows")),
        P(("groups", "cols")),
        P(("groups", "cols")),
        P(("groups", "rows")),
        P(None, "rows"),
        P(None, "rhs"),
        P("rhs"),
        P("rhs", "rows"),
    )
    out_specs = (P("rhs", ("groups", "rows", "cols")), P("rhs", ("groups", "rows", "cols")))
    return jax.shard_map(
        per_device, mesh=mesh, in_specs=in_specs, out_specs=out_specs, check_vma=False
    )
```

```python
import functools

import jax
import jax.numpy as jnp
from jax import lax
from jax.experimental import pallas as pl
from jax.experimental.pallas import tpu as pltpu
from jax.sharding import PartitionSpec as P

BLOCK = 8
LANES = 128
SHIFT = 3.0
GRID = ("rows", "cols", "rhs")
F32 = jnp.float32
BF16 = jnp.bfloat16

VMEM = pl.BlockSpec(memory_space=pltpu.VMEM)
SMEM = pl.BlockSpec(memory_space=pltpu.SMEM)
ANY = pl.BlockSpec(memory_space=pl.ANY)

CORE, CHUNKS = 0, 1


def dot(left, right, dims):
    return lax.dot_general(left, right, (dims, ((), ())), preferred_element_type=F32)


def precise(left, right, dims):
    return lax.dot_general(
        left, right, (dims, ((), ())), precision=lax.Precision.HIGHEST, preferred_element_type=F32
    )


def low_onehot(index):
    low = jnp.bitwise_and(index, LANES - 1)
    hit = lax.broadcasted_iota(jnp.int32, (LANES, index.shape[1]), 0) == low
    return jnp.where(hit, 1.0, 0.0).astype(BF16)


def take_columns(field, index):
    rows, width = field.shape
    chunks = width // LANES
    stacked = jnp.concatenate(
        [field[:, i * LANES : (i + 1) * LANES] for i in range(chunks)], axis=0
    )
    picked = dot(stacked, low_onehot(index), ((1,), (0,)))
    high = jnp.right_shift(index, 7)
    total = jnp.zeros((rows, index.shape[1]), F32)
    for i in range(chunks):
        total = total + jnp.where(high == i, picked[i * rows : (i + 1) * rows], 0.0)
    return total


def put_columns(values, index, width):
    rows = values.shape[0]
    chunks = width // LANES
    upper = values.astype(BF16).astype(F32)
    parts = (upper, values - upper)
    high = jnp.right_shift(index, 7)
    onehot = low_onehot(index)
    total = None
    for part in parts:
        stacked = jnp.concatenate(
            [jnp.where(high == i, part, 0.0).astype(BF16) for i in range(chunks)], axis=0
        )
        spread = dot(stacked, onehot, ((1,), (1,)))
        total = spread if total is None else total + spread
    return jnp.concatenate([total[i * rows : (i + 1) * rows] for i in range(chunks)], axis=1)


def both_cores(core, own, other):
    first = jnp.where(core == 0, own, other)
    second = jnp.where(core == 0, other, own)
    return jnp.concatenate([first, second], axis=0)


def load_copies(influence, wake, held, sems, first, base, chunk):
    def copies(i):
        source = pl.ds(pl.multiple_of(first + base + i * chunk, 16), chunk)
        target = pl.ds(i * chunk, chunk)
        panels = influence.shape[1]
        return (
            pltpu.make_async_copy(
                influence.at[source], held.at[target, pl.ds(0, panels)], sems.at[0, i]
            ),
            pltpu.make_async_copy(
                wake.at[source], held.at[target, pl.ds(panels, wake.shape[1])], sems.at[1, i]
            ),
        )

    return copies


def right_kernel(
    chunk, half, scalars, pitch, pitch_other, modes, modes_other, blade, shapes, influence, wake,
    right, gram, held, sems
):
    core = scalars[CORE]
    copies = load_copies(influence, wake, held, sems, core * half, 0, chunk)
    steps = held.shape[0] // chunk
    for i in range(steps):
        for copy in copies(i):
            copy.start()
    blades = pitch.shape[0]
    blade_onehot = jnp.where(
        lax.broadcasted_iota(jnp.int32, (blades, blade.shape[1]), 0) == blade[...], 1.0, 0.0
    )
    for b in range(2):
        own = core == b
        amount = jnp.where(own, pitch[...], pitch_other[...])
        mode = jnp.where(own, modes[...], modes_other[...])
        mode_onehot = jnp.where(
            lax.broadcasted_iota(jnp.int32, (shapes.shape[0], BLOCK), 0) == mode, 1.0, 0.0
        )
        pattern = precise(mode_onehot, shapes[...], ((0,), (0,)))
        factor = precise(amount, blade_onehot, ((0,), (0,)))
        right[b * BLOCK : (b + 1) * BLOCK, :] = pattern * factor
    gram[...] = precise(right[...], right[...], ((1,), (1,)))
    for i in range(steps):
        for copy in copies(i):
            copy.wait()


def finish_adjoint(scalars, upper, lower, whole, keep, give):
    piece = keep.shape[1]
    panels = 2 * piece
    carried = whole[:, panels:]
    whole[:, 0:panels] += put_columns(carried, upper[...], panels) - put_columns(
        carried, lower[...], panels
    )
    core = scalars[CORE]
    keep[...] = whole[:, pl.ds(pl.multiple_of(core * piece, LANES), piece)]
    give[...] = whole[:, pl.ds(pl.multiple_of((1 - core) * piece, LANES), piece)]


def load_adjoint_kernel(
    chunk, scalars, objectives, objectives_other, self_term, upper, lower, held_first, influence,
    wake, keep, give, start, target, self_half, held, whole, sems
):
    half = start.shape[1]
    first_rows = held_first.shape[0]
    core = scalars[CORE]
    copies = load_copies(influence, wake, held, sems, core * half, first_rows, chunk)
    steps = held.shape[0] // chunk
    for i in range(steps):
        for copy in copies(i):
            copy.start()
    span = pl.ds(pl.multiple_of(core * half, LANES), half)
    target[...] = both_cores(core, objectives[:, span], objectives_other[:, span])
    self_half[...] = self_term[:, span]
    start[...] = target[...] / self_half[...]
    field = start[...].astype(BF16)
    whole[...] = dot(field[:, 0:first_rows], held_first[...], ((1,), (0,)))
    for i in range(steps):
        for copy in copies(i):
            copy.wait()
        begin = first_rows + i * chunk
        whole[...] += dot(
            field[:, begin : begin + chunk],
            held[i * chunk : (i + 1) * chunk, :],
            ((1,), (0,)),
        )
    finish_adjoint(scalars, upper, lower, whole, keep, give)


def adjoint_kernel(
    tile, n_in, scalars, previous, target, self_half, upper, lower, held_first, held, *rest
):
    parts, (keep, give, adjoint, whole) = rest[:n_in], rest[n_in:]
    image = self_half[...] * previous[...]
    for part in parts:
        image = image + part[...].astype(F32)
    adjoint[...] = previous[...] + (target[...] - image) / self_half[...]
    field = adjoint[...].astype(BF16)
    width = held.shape[1]
    first_rows = held_first.shape[0]
    for start in range(0, width, tile):
        stop = min(width, start + tile)
        whole[:, start:stop] = dot(
            field[:, 0:first_rows], held_first[:, start:stop], ((1,), (0,))
        ) + dot(field[:, first_rows:], held[:, start:stop], ((1,), (0,)))
    finish_adjoint(scalars, upper, lower, whole, keep, give)


def forward_kernel(tile, places, scalars, upper, lower, held_first, held, *rest):
    shards, (out, field) = rest[: len(places)], rest[len(places) :]
    for place, ref in zip(places, shards):
        begin = pl.multiple_of(scalars[place], LANES)
        field[:, pl.ds(begin, ref.shape[1])] = ref[...]
    panels = held.shape[1] - upper.shape[1]
    source = field[:, 0:panels]
    strength = take_columns(source, upper[...]) - take_columns(source, lower[...])
    field[:, panels:] = strength.astype(BF16)
    base = 0
    for part in (held_first, held):
        for start in range(0, part.shape[0], tile):
            stop = min(part.shape[0], start + tile)
            out[:, base + start : base + stop] = dot(
                field[...], part[start:stop, :], ((1,), (1,))
            )
        base += part.shape[0]


def inverse_factor(gram):
    size = gram.shape[0]
    row = lax.broadcasted_iota(jnp.int32, (size, size), 0)
    col = lax.broadcasted_iota(jnp.int32, (size, size), 1)
    left = jnp.where(row == col, 1.0, 0.0)
    for j in range(size - 1):
        scale = jnp.where(
            row[:, 0:1] > j, gram[:, j : j + 1] / gram[j : j + 1, j : j + 1], 0.0
        )
        left = left - scale * left[j : j + 1, :]
        gram = gram - scale * gram[j : j + 1, :]
    pivots = jnp.sum(jnp.where(row == col, gram, 0.0), axis=1, keepdims=True)
    return left / jnp.sqrt(pivots)


def start_kernel(n_parts, scalars, right_piece, right, *rest):
    parts, (rounded, basis, right_half) = rest[:n_parts], rest[n_parts:]
    half = basis.shape[1]
    span = pl.ds(pl.multiple_of(scalars[CORE] * half, LANES), half)
    gram = parts[0][...]
    for part in parts[1:]:
        gram = gram + part[...]
    right_half[...] = right[:, span]
    for b in range(gram.shape[0] // BLOCK):
        rows = slice(b * BLOCK, (b + 1) * BLOCK)
        inverse = inverse_factor(gram[rows, rows])
        rounded[rows, :] = precise(inverse, right_piece[rows, :], ((1,), (0,))).astype(BF16)
        basis[rows, :] = precise(inverse, right_half[rows, :], ((1,), (0,)))


def system_kernel(n_parts, scalars, basis, image, right, self_half, *rest):
    parts, (keep, give) = rest[:n_parts], rest[n_parts:]
    second = self_half[...] * image[...]
    for part in parts:
        second = second + part[...]
    first = image[...] + SHIFT * basis[...]
    core = scalars[CORE]
    keep[...] = jnp.zeros_like(keep)
    give[...] = jnp.zeros_like(give)
    for b in range(2):
        rows = slice(b * BLOCK, (b + 1) * BLOCK)
        images = jnp.concatenate([first[rows], second[rows]], axis=0)
        full = jnp.concatenate([images, right[rows, :]], axis=0)
        system = precise(images, full, ((1,), (1,)))
        size = system.shape[1]

        @pl.when(core == b)
        def _():
            keep[:, 0:size] = system

        @pl.when(core != b)
        def _():
            give[:, 0:size] = system


def solve_kernel(n_parts, basis, *rest):
    parts, out = rest[:n_parts], rest[n_parts]
    system = parts[0][...]
    for part in parts[1:]:
        system = system + part[...]
    size = basis.shape[0]
    row = lax.broadcasted_iota(jnp.int32, (size, 1), 0)
    for j in range(size):
        pivot_row = system[j : j + 1, :] / system[j : j + 1, j : j + 1]
        factor = jnp.where(row == j, 0.0, system[:, j : j + 1])
        system = jnp.where(row == j, pivot_row, system - factor * pivot_row)
    weights = system[:, size : size + BLOCK]
    out[...] = precise(weights, basis[...], ((0,), (0,)))


def params(mib=20):
    return pltpu.CompilerParams(vmem_limit_bytes=mib << 20)


def cost(flops, size):
    return pl.CostEstimate(flops=flops, bytes_accessed=size, transcendentals=0)


def per_device(
    influence,
    wake_influence,
    self_term,
    wake_upper,
    wake_lower,
    blade_of,
    mode_shapes,
    blade_pitch,
    design_map,
    objectives,
):
    influence = pltpu.with_memory_space_constraint(influence, pltpu.HBM)
    wake_influence = pltpu.with_memory_space_constraint(wake_influence, pltpu.HBM)
    n_rows, n_cols, n_rhs = (lax.axis_size(name) for name in GRID)
    side = n_cols * n_rhs
    piece, panels = influence.shape
    wake = wake_influence.shape[1]
    half = piece // n_rhs
    out_width = piece // n_cols
    count = 2 * BLOCK
    width = panels + wake
    if n_rows != side or n_rhs != 2 or panels != 2 * piece:
        raise ValueError("unsupported mesh")
    row_index = lax.axis_index("rows")
    col_index = lax.axis_index("cols")
    core = lax.axis_index("rhs")

    def cross(k):
        return [(a * side + b, b * side + (a ^ k)) for a in range(side) for b in range(side)]

    def fetch(j):
        return [
            (a * side + c * n_rhs + h, ((h ^ j) * n_cols + c) * side + a)
            for a in range(side)
            for c in range(n_cols)
            for h in range(n_rhs)
        ]

    def flip(k, size):
        return [(i, i ^ k) for i in range(size)]

    def swap(value):
        return lax.ppermute(value, "rhs", flip(1, 2))

    def cols_parts(value):
        return [value] + [lax.ppermute(value, "cols", flip(k, n_cols)) for k in range(1, n_cols)]

    near = core * piece
    far = (1 - core) * piece
    chunk_half = row_index // n_cols
    places = [
        near + chunk_half * half,
        near + (1 - chunk_half) * half,
        far + chunk_half * half,
        far + (1 - chunk_half) * half,
        near,
        far,
    ]
    scalars = jnp.stack([core] + places).astype(jnp.int32)
    col_start = col_index * panels
    local_upper = (wake_upper - col_start)[None, :]
    local_lower = (wake_lower - col_start)[None, :]
    self_row = self_term[None, :]

    first_rows = half // 4
    chunk = half // 8
    struct = jax.ShapeDtypeStruct

    modes = design_map[None, :]
    objectives_other = swap(objectives)
    right, gram, held_first = pl.pallas_call(
        functools.partial(right_kernel, chunk, half),
        in_specs=[SMEM] + [VMEM] * 6 + [ANY, ANY],
        out_specs=[VMEM] * 3,
        out_shape=[
            struct((count, piece), F32),
            struct((count, count), F32),
            pltpu.VMEM((first_rows, width), BF16),
        ],
        scratch_shapes=[pltpu.SemaphoreType.DMA((2, first_rows // chunk))],
        compiler_params=params(),
        cost_estimate=cost(0, 2 * first_rows * width),
        name="right",
    )(
        scalars, blade_pitch, swap(blade_pitch), modes, swap(modes), blade_of[None, :], mode_shapes,
        influence, wake_influence,
    )
    right_piece = lax.ppermute(right, GRID, cross(0))
    grams = [gram] + [lax.ppermute(gram, "rows", flip(k, n_rows)) for k in range(1, n_rows)]

    held_first = pltpu.with_memory_space_constraint(held_first, pltpu.VMEM)
    rest_rows = half - first_rows
    keep, give, start, target, self_half, held = pl.pallas_call(
        functools.partial(load_adjoint_kernel, chunk),
        in_specs=[SMEM] + [VMEM] * 6 + [ANY, ANY],
        out_specs=[VMEM] * 6,
        out_shape=[
            struct((count, piece), F32),
            struct((count, piece), F32),
            struct((count, half), F32),
            struct((count, half), F32),
            struct((1, half), F32),
            pltpu.VMEM((rest_rows, width), BF16),
        ],
        scratch_shapes=[
            pltpu.VMEM((count, width), F32),
            pltpu.SemaphoreType.DMA((2, rest_rows // chunk)),
        ],
        compiler_params=params(),
        cost_estimate=cost(2 * count * half * width, 2 * rest_rows * width),
        name="adjoint_one",
    )(
        scalars, objectives, objectives_other, self_row, local_upper, local_lower, held_first,
        influence, wake_influence,
    )
    held = pltpu.with_memory_space_constraint(held, pltpu.VMEM)
    product_cost = cost(2 * count * half * width, 2 * half * width)

    def forward(places, shards, name):
        return pl.pallas_call(
            functools.partial(forward_kernel, 512, places),
            in_specs=[SMEM] + [VMEM] * (4 + len(shards)),
            out_specs=VMEM,
            out_shape=struct((count, half), F32),
            scratch_shapes=[pltpu.VMEM((count, width), BF16)],
            compiler_params=params(),
            cost_estimate=product_cost,
            name=name,
        )(scalars, local_upper, local_lower, held_first, held, *shards)

    rounded, basis, right_half = pl.pallas_call(
        functools.partial(start_kernel, len(grams)),
        in_specs=[SMEM] + [VMEM] * (2 + len(grams)),
        out_specs=[VMEM] * 3,
        out_shape=[
            struct((count, piece), BF16),
            struct((count, half), F32),
            struct((count, half), F32),
        ],
        compiler_params=params(),
        name="start",
    )(scalars, right_piece, right, *grams)
    induced = forward((CHUNKS + 4, CHUNKS + 5), [rounded, swap(rounded)], "forward_one")

    total = keep + swap(give)
    sides = total[:, :half].astype(BF16), total[:, half:].astype(BF16)
    odd = row_index % 2 == 1
    sends = jnp.where(odd, sides[1], sides[0]), jnp.where(odd, sides[0], sides[1])
    parts = [lax.ppermute(sends[k % 2], GRID, cross(k)) for k in range(side)]

    image = sum(cols_parts(induced)) + (self_half - SHIFT) * basis
    image_rounded = image.astype(BF16)

    keep, give, adjoint = pl.pallas_call(
        functools.partial(adjoint_kernel, 512, len(parts)),
        in_specs=[SMEM] + [VMEM] * (7 + len(parts)),
        out_specs=[VMEM] * 3,
        out_shape=[
            struct((count, piece), F32),
            struct((count, piece), F32),
            struct((count, half), F32),
        ],
        scratch_shapes=[pltpu.VMEM((count, width), F32)],
        compiler_params=params(),
        cost_estimate=product_cost,
        name="adjoint_two",
    )(scalars, start, target, self_half, local_upper, local_lower, held_first, held, *parts)

    shards = [lax.ppermute(image_rounded, GRID, fetch(j)) for j in range(2)]
    shards = shards + [swap(value) for value in shards]
    induced = forward(tuple(CHUNKS + i for i in range(4)), shards, "forward_two")

    induced = cols_parts(induced)
    system_keep, system_give = pl.pallas_call(
        functools.partial(system_kernel, len(induced)),
        in_specs=[SMEM] + [VMEM] * (4 + len(induced)),
        out_specs=[VMEM] * 2,
        out_shape=[struct((count, LANES), F32)] * 2,
        compiler_params=params(),
        name="system",
    )(scalars, basis, image, right_half, self_half, *induced)
    system = system_keep + swap(system_give)
    systems = [system] + [lax.ppermute(system, "rows", flip(k, n_rows)) for k in range(1, n_rows)]

    begin = col_index * out_width
    holder = begin // half
    begin = begin % half

    def to_output(*values):
        mine = [lax.dynamic_slice_in_dim(value, begin, out_width, 1) for value in values]

        def rows(which):
            return jnp.concatenate(
                [lax.dynamic_slice_in_dim(v, which * BLOCK, BLOCK, 0) for v in mine], axis=0
            )

        return jnp.where(core == holder, rows(core), swap(rows(1 - core)))

    bases = to_output(basis, image)
    solution = pl.pallas_call(
        functools.partial(solve_kernel, len(systems)),
        in_specs=[VMEM] * (1 + len(systems)),
        out_specs=VMEM,
        out_shape=struct((BLOCK, out_width), F32),
        compiler_params=params(),
        name="solve",
    )(bases, *systems)

    total = keep + swap(give)
    previous = to_output(adjoint)
    span = col_index * out_width
    self_out = lax.dynamic_slice_in_dim(self_term, span, out_width, 0)[None, :]
    target_out = lax.dynamic_slice_in_dim(objectives, span, out_width, 1)
    image = self_out * previous
    for k in range(side):
        goal = jnp.bitwise_xor(row_index, k)
        part = lax.dynamic_slice(
            total, ((goal % n_rhs) * BLOCK, (goal // n_rhs) * out_width), (BLOCK, out_width)
        )
        image = image + lax.ppermute(part, GRID, cross(k))
    adjoint = previous + (target_out - image) / self_out
    return (solution, adjoint)


def solution(mesh):
    in_specs = (
        P(("groups", "rows"), "cols"),
        P(("groups", "rows"), "cols"),
        P(("groups", "rows")),
        P(("groups", "cols")),
        P(("groups", "cols")),
        P(("groups", "rows")),
        P(None, "rows"),
        P(None, "rhs"),
        P("rhs"),
        P("rhs", "rows"),
    )
    out_specs = (P("rhs", ("groups", "rows", "cols")), P("rhs", ("groups", "rows", "cols")))
    return jax.shard_map(
        per_device, mesh=mesh, in_specs=in_specs, out_specs=out_specs, check_vma=False
    )
```

```python
import functools

import jax
import jax.numpy as jnp
from jax import lax
from jax.experimental import pallas as pl
from jax.experimental.pallas import tpu as pltpu
from jax.sharding import PartitionSpec as P

BLOCK = 8
LANES = 128
SHIFT = 3.0
GRID = ("rows", "cols", "rhs")
F32 = jnp.float32
BF16 = jnp.bfloat16

VMEM = pl.BlockSpec(memory_space=pltpu.VMEM)
SMEM = pl.BlockSpec(memory_space=pltpu.SMEM)
ANY = pl.BlockSpec(memory_space=pl.ANY)

CORE, COLUMNS, ROW, BEGIN, HOLDER, SPAN, CHUNKS = range(7)


def dot(left, right, dims):
    return lax.dot_general(left, right, (dims, ((), ())), preferred_element_type=F32)


def precise(left, right, dims):
    return lax.dot_general(
        left, right, (dims, ((), ())), precision=lax.Precision.HIGHEST, preferred_element_type=F32
    )


def low_onehot(index):
    low = jnp.bitwise_and(index, LANES - 1)
    hit = lax.broadcasted_iota(jnp.int32, (LANES, index.shape[1]), 0) == low
    return jnp.where(hit, 1.0, 0.0).astype(BF16)


def take_columns(field, index):
    rows, width = field.shape
    chunks = width // LANES
    stacked = jnp.concatenate(
        [field[:, i * LANES : (i + 1) * LANES] for i in range(chunks)], axis=0
    )
    picked = dot(stacked, low_onehot(index), ((1,), (0,)))
    high = jnp.right_shift(index, 7)
    total = jnp.zeros((rows, index.shape[1]), F32)
    for i in range(chunks):
        total = total + jnp.where(high == i, picked[i * rows : (i + 1) * rows], 0.0)
    return total


def put_columns(values, index, width):
    rows = values.shape[0]
    chunks = width // LANES
    high = jnp.right_shift(index, 7)
    stacked = jnp.concatenate(
        [jnp.where(high == i, values, 0.0).astype(BF16) for i in range(chunks)], axis=0
    )
    spread = dot(stacked, low_onehot(index), ((1,), (1,)))
    return jnp.concatenate([spread[i * rows : (i + 1) * rows] for i in range(chunks)], axis=1)


def both_cores(core, own, other):
    first = jnp.where(core == 0, own, other)
    second = jnp.where(core == 0, other, own)
    return jnp.concatenate([first, second], axis=0)


def load_copies(influence, wake, held, sems, first, chunk):
    def copies(i):
        source = pl.ds(pl.multiple_of(first + i * chunk, 16), chunk)
        target = pl.ds(i * chunk, chunk)
        panels = influence.shape[1]
        return (
            pltpu.make_async_copy(
                influence.at[source], held.at[target, pl.ds(0, panels)], sems.at[0, i]
            ),
            pltpu.make_async_copy(
                wake.at[source], held.at[target, pl.ds(panels, wake.shape[1])], sems.at[1, i]
            ),
        )

    return copies


def right_kernel(
    half, scalars, pitch, pitch_other, modes, modes_other, blade, shapes, right, right_half
):
    core = scalars[CORE]
    blades = pitch.shape[0]
    blade_onehot = jnp.where(
        lax.broadcasted_iota(jnp.int32, (blades, blade.shape[1]), 0) == blade[...], 1.0, 0.0
    )
    for b in range(2):
        own = core == b
        amount = jnp.where(own, pitch[...], pitch_other[...])
        mode = jnp.where(own, modes[...], modes_other[...])
        mode_onehot = jnp.where(
            lax.broadcasted_iota(jnp.int32, (shapes.shape[0], BLOCK), 0) == mode, 1.0, 0.0
        )
        pattern = precise(mode_onehot, shapes[...], ((0,), (0,)))
        factor = precise(amount, blade_onehot, ((0,), (0,)))
        right[b * BLOCK : (b + 1) * BLOCK, :] = pattern * factor
    right_half[...] = right[:, pl.ds(pl.multiple_of(core * half, LANES), half)]


def local_wake(scalars, upper, lower):
    start = scalars[COLUMNS]
    return upper[...] - start, lower[...] - start


def load_first_kernel(
    chunk, steps, scalars, objectives, objectives_other, self_term, influence, wake,
    start, target, self_half, whole, held, sems
):
    half = start.shape[1]
    core = scalars[CORE]
    copies = load_copies(influence, wake, held, sems, core * half, chunk)
    for i in range(steps):
        for copy in copies(i):
            copy.start()
    span = pl.ds(pl.multiple_of(core * half, LANES), half)
    target[...] = both_cores(core, objectives[:, span], objectives_other[:, span])
    self_half[...] = self_term[:, span]
    start[...] = target[...] / self_half[...]
    for i in range(steps):
        for copy in copies(i):
            copy.wait()
        rows = slice(i * chunk, (i + 1) * chunk)
        part = dot(start[:, rows].astype(BF16), held[rows, :], ((1,), (0,)))
        if i == 0:
            whole[...] = part
        else:
            whole[...] += part


def load_rest_kernel(
    chunk, steps, scalars, start, upper, lower, whole_first, influence, wake, held_first,
    keep, give, held, whole, sems
):
    half = start.shape[1]
    piece = keep.shape[1]
    panels = 2 * piece
    core = scalars[CORE]
    copies = load_copies(influence, wake, held, sems, core * half, chunk)
    for i in range(*steps):
        for copy in copies(i):
            copy.start()
    whole[...] = whole_first[...]
    for i in range(*steps):
        for copy in copies(i):
            copy.wait()
        rows = slice(i * chunk, (i + 1) * chunk)
        whole[...] += dot(start[:, rows].astype(BF16), held[rows, :], ((1,), (0,)))
    upper_local, lower_local = local_wake(scalars, upper, lower)
    carried = whole[:, panels:]
    whole[:, 0:panels] += put_columns(carried, upper_local, panels) - put_columns(
        carried, lower_local, panels
    )
    keep[...] = whole[:, pl.ds(pl.multiple_of(core * piece, LANES), piece)]
    give[...] = whole[:, pl.ds(pl.multiple_of((1 - core) * piece, LANES), piece)]


def adjoint_piece(tile, scalars, field, which, carried, upper, lower, held, out):
    width = out.shape[1]
    piece = out.shape[0] // (2 * BLOCK) * width
    begin = which * piece
    upper_local, lower_local = local_wake(scalars, upper, lower)
    spread = put_columns(carried, upper_local - begin, piece) - put_columns(
        carried, lower_local - begin, piece
    )
    for start in range(0, piece, tile):
        span = pl.ds(pl.multiple_of(begin + start, LANES), tile)
        part = (
            dot(field, held[:, span], ((1,), (0,)))
            + spread[:, start : start + tile]
        )
        col, offset = divmod(start, width)
        for b in range(2):
            goal = (col * 2 + b) * BLOCK
            out[goal : goal + BLOCK, offset : offset + tile] = part[b * BLOCK : (b + 1) * BLOCK]


def adjoint_give_kernel(
    tile, n_in, scalars, previous, target, self_half, upper, lower, held, *rest
):
    parts, (give, adjoint, carried, mine, send) = rest[:n_in], rest[n_in:]
    image = self_half[...] * previous[...]
    for part in parts:
        image = image + part[...].astype(F32)
    adjoint[...] = previous[...] + (target[...] - image) / self_half[...]
    to_output(scalars, (adjoint,), mine, send)
    field = adjoint[...].astype(BF16)
    panels = held.shape[1] - carried.shape[1]
    carried[...] = dot(field, held[:, panels:], ((1,), (0,)))
    which = 1 - scalars[CORE]
    adjoint_piece(
        tile, scalars, field, which, carried[...], upper, lower, held, give
    )


def adjoint_keep_kernel(
    tile, scalars, adjoint, carried, upper, lower, held, ready, keep
):
    field = adjoint[...].astype(BF16)
    which = scalars[CORE]
    adjoint_piece(
        tile, scalars, field, which, carried[...], upper, lower, held, keep
    )


def forward_kernel(tile, places, split, scalars, upper, lower, held, *rest):
    shards, (out, field) = rest[: len(places)], rest[len(places) :]
    count = out.shape[0]
    for place, ref in zip(places, shards):
        span = pl.ds(pl.multiple_of(scalars[place], LANES), ref.shape[1])
        if split:
            high = ref[...].astype(BF16)
            field[0:count, span] = high
            field[count:, span] = (ref[...] - high.astype(F32)).astype(BF16)
        else:
            field[:, span] = ref[...]
    panels = held.shape[1] - upper.shape[1]
    source = field[:, 0:panels]
    upper_local, lower_local = local_wake(scalars, upper, lower)
    strength = take_columns(source, upper_local) - take_columns(source, lower_local)
    if split:
        strength = strength[0:count] + strength[count:]
        high = strength.astype(BF16)
        field[0:count, panels:] = high
        field[count:, panels:] = (strength - high.astype(F32)).astype(BF16)
    else:
        field[:, panels:] = strength.astype(BF16)
    for start in range(0, held.shape[0], tile):
        result = dot(field[...], held[start : start + tile, :], ((1,), (1,)))
        if split:
            result = result[0:count] + result[count:]
        out[:, start : start + tile] = result


def system_kernel(n_parts, scalars, basis, image, self_half, *rest):
    parts, (keep, give) = rest[:n_parts], rest[n_parts:]
    second = self_half[...] * image[...]
    for part in parts:
        second = second + part[...]
    first = image[...] + SHIFT * basis[...]
    core = scalars[CORE]
    keep[...] = jnp.zeros_like(keep)
    give[...] = jnp.zeros_like(give)
    for b in range(2):
        rows = slice(b * BLOCK, (b + 1) * BLOCK)
        images = jnp.concatenate([first[rows], second[rows]], axis=0)
        full = jnp.concatenate([images, basis[rows, :]], axis=0)
        system = precise(images, full, ((1,), (1,)))
        size = system.shape[1]

        @pl.when(core == b)
        def _():
            keep[:, 0:size] = system

        @pl.when(core != b)
        def _():
            give[:, 0:size] = system


def to_output(scalars, values, mine, send):
    width = mine.shape[1]
    core = scalars[CORE]
    span = pl.ds(pl.multiple_of(scalars[BEGIN], LANES), width)
    for i, value in enumerate(values):
        first = value[0:BLOCK, span]
        second = value[BLOCK : 2 * BLOCK, span]
        rows = slice(i * BLOCK, (i + 1) * BLOCK)
        mine[rows, :] = jnp.where(core == 0, first, second)
        send[rows, :] = jnp.where(core == 0, second, first)


def combine_kernel(scalars, keep, other, first, second):
    half = first.shape[1]
    low = (keep[:, 0:half] + other[:, 0:half]).astype(BF16)
    high = (keep[:, half:] + other[:, half:]).astype(BF16)
    odd = scalars[ROW] % 2 == 1
    first[...] = jnp.where(odd, high, low)
    second[...] = jnp.where(odd, low, high)


def image_kernel(n_parts, scalars, right_half, self_half, *rest):
    parts, (image, rounded, mine, send) = rest[:n_parts], rest[n_parts:]
    total = (self_half[...] - SHIFT) * right_half[...]
    for part in parts:
        total = total + part[...]
    image[...] = total
    rounded[...] = total.astype(BF16)
    to_output(scalars, (right_half, image), mine, send)


def collect_kernel(scalars, keep, other, ready, *outs):
    for k, out in enumerate(outs):
        rows = pl.ds(pl.multiple_of(jnp.bitwise_xor(scalars[ROW], k) * BLOCK, BLOCK), BLOCK)
        out[...] = keep[rows, :] + other[rows, :]


def update_kernel(n_parts, scalars, mine, received, self_term, objectives, *rest):
    parts, out = rest[:n_parts], rest[n_parts]
    span = pl.ds(pl.multiple_of(scalars[SPAN], LANES), out.shape[1])
    previous = jnp.where(scalars[HOLDER] == 1, mine[...], received[...])
    scale = self_term[:, span]
    image = scale * previous
    for part in parts:
        image = image + part[...]
    out[...] = previous + (objectives[:, span] - image) / scale


def solve_kernel(n_parts, scalars, mine, received, *rest):
    parts, out = rest[:n_parts], rest[n_parts]
    basis = jnp.where(scalars[HOLDER] == 1, mine[...], received[...])
    system = parts[0][...]
    for part in parts[1:]:
        system = system + part[...]
    size = basis.shape[0]
    row = lax.broadcasted_iota(jnp.int32, (size, 1), 0)
    for j in range(size):
        pivot_row = system[j : j + 1, :] / system[j : j + 1, j : j + 1]
        factor = jnp.where(row == j, 0.0, system[:, j : j + 1])
        system = jnp.where(row == j, pivot_row, system - factor * pivot_row)
    weights = system[:, size : size + BLOCK]
    out[...] = precise(weights, basis, ((0,), (0,)))


def argument(value):
    return pltpu.with_memory_space_constraint(value, pltpu.HBM)


def keep_in_vmem(value):
    return pltpu.with_memory_space_constraint(value, pltpu.VMEM)


def params(mib=20):
    return pltpu.CompilerParams(vmem_limit_bytes=mib << 20)


def cost(flops, size):
    return pl.CostEstimate(flops=flops, bytes_accessed=size, transcendentals=0)


def per_device(
    influence,
    wake_influence,
    self_term,
    wake_upper,
    wake_lower,
    blade_of,
    mode_shapes,
    blade_pitch,
    design_map,
    objectives,
):
    influence = argument(influence)
    wake_influence = argument(wake_influence)
    n_rows, n_cols, n_rhs = (lax.axis_size(name) for name in GRID)
    side = n_cols * n_rhs
    piece, panels = influence.shape
    wake = wake_influence.shape[1]
    half = piece // n_rhs
    out_width = piece // n_cols
    count = 2 * BLOCK
    width = panels + wake
    if n_rows != side or n_rhs != 2 or panels != 2 * piece:
        raise ValueError("unsupported mesh")
    row_index = lax.axis_index("rows")
    col_index = lax.axis_index("cols")
    core = lax.axis_index("rhs")

    def cross(k):
        return [(a * side + b, b * side + (a ^ k)) for a in range(side) for b in range(side)]

    def fetch(j):
        return [
            (a * side + c * n_rhs + h, ((h ^ j) * n_cols + c) * side + a)
            for a in range(side)
            for c in range(n_cols)
            for h in range(n_rhs)
        ]

    def flip(k, size):
        return [(i, i ^ k) for i in range(size)]

    def swap(value):
        return lax.ppermute(value, "rhs", flip(1, 2))

    def cols_parts(value):
        return [value] + [lax.ppermute(value, "cols", flip(k, n_cols)) for k in range(1, n_cols)]

    near = core * piece
    far = (1 - core) * piece
    chunk_half = row_index // n_cols
    places = [
        near + chunk_half * half,
        near + (1 - chunk_half) * half,
        far + chunk_half * half,
        far + (1 - chunk_half) * half,
        near,
        far,
    ]
    span = col_index * out_width
    holder = (core == span // half).astype(jnp.int32)
    scalars = jnp.stack(
        [core, col_index * panels, row_index, span % half, holder, span] + places
    ).astype(jnp.int32)
    self_row = argument(self_term[None, :])
    objectives = argument(objectives)
    upper = argument(wake_upper[None, :])
    lower = argument(wake_lower[None, :])

    first_rows = half // 2
    parts_first, parts_all = first_rows // (half // 8), 8
    chunk = half // 8
    struct = jax.ShapeDtypeStruct

    modes = design_map[None, :]
    objectives_other = swap(objectives)
    right, right_half = pl.pallas_call(
        functools.partial(right_kernel, half),
        in_specs=[SMEM] + [VMEM] * 6,
        out_specs=[VMEM] * 2,
        out_shape=[struct((count, piece), F32), struct((count, half), F32)],
        compiler_params=params(4),
        name="right",
    )(
        scalars, argument(blade_pitch), (swap(blade_pitch)), argument(modes),
        (swap(modes)),
        argument(blade_of[None, :]), argument(mode_shapes),
    )
    right_near = lax.ppermute(right, GRID, cross(0))

    start, target, self_half, whole, held = pl.pallas_call(
        functools.partial(load_first_kernel, chunk, parts_first),
        in_specs=[SMEM] + [VMEM] * 3 + [ANY, ANY],
        out_specs=[VMEM] * 5,
        out_shape=[
            struct((count, half), F32),
            struct((count, half), F32),
            struct((1, half), F32),
            struct((count, width), F32),
            pltpu.VMEM((half, width), BF16),
        ],
        scratch_shapes=[pltpu.SemaphoreType.DMA((2, parts_first))],
        compiler_params=params(),
        cost_estimate=cost(count * half * width, 2 * first_rows * width),
        name="adjoint_one_first",
    )(
        scalars, objectives, objectives_other, self_row, influence,
        wake_influence,
    )
    right_near, start = lax.optimization_barrier((right_near, start))
    right_far = swap(right_near)
    keep, give, held = pl.pallas_call(
        functools.partial(load_rest_kernel, chunk, (parts_first, parts_all)),
        in_specs=[SMEM] + [VMEM] * 4 + [ANY, ANY, VMEM],
        out_specs=[VMEM] * 3,
        out_shape=[
            struct((count, piece), F32),
            struct((count, piece), F32),
            pltpu.VMEM((half, width), BF16),
        ],
        scratch_shapes=[
            pltpu.VMEM((count, width), F32),
            pltpu.SemaphoreType.DMA((2, parts_all)),
        ],
        compiler_params=params(),
        input_output_aliases={7: 2},
        cost_estimate=cost(count * half * width, half * width),
        name="adjoint_one_rest",
    )(
        scalars, start, upper, lower, whole, influence, wake_influence,
        keep_in_vmem(held),
    )
    held = keep_in_vmem(held)

    def forward(places, shards, split, name):
        rows = 2 * count if split else count
        return pl.pallas_call(
            functools.partial(forward_kernel, 512, places, split),
            in_specs=[SMEM] + [VMEM] * (3 + len(shards)),
            out_specs=VMEM,
            out_shape=struct((count, half), F32),
            scratch_shapes=[pltpu.VMEM((rows, width), BF16)],
            compiler_params=params(),
            cost_estimate=cost(2 * count * half * width, 2 * half * width),
            name=name,
        )(scalars, upper, lower, held, *shards)

    sends = pl.pallas_call(
        combine_kernel,
        in_specs=[SMEM] + [VMEM] * 2,
        out_specs=[VMEM] * 2,
        out_shape=[struct((count, half), BF16)] * 2,
        compiler_params=params(4),
        name="combine",
    )(scalars, keep, swap(give))

    right_far, *sends = lax.optimization_barrier((right_far, *sends))
    induced = forward(
        (CHUNKS + 4, CHUNKS + 5), [right_near, right_far], True, "forward_one"
    )
    parts = [lax.ppermute(sends[k % 2], GRID, cross(k)) for k in range(side)]
    induced, *parts = lax.optimization_barrier((induced, *parts))

    tile = min(512, out_width)
    give, adjoint, carried, adjoint_mine, adjoint_send = pl.pallas_call(
        functools.partial(adjoint_give_kernel, tile, len(parts)),
        in_specs=[SMEM] + [VMEM] * (6 + len(parts)),
        out_specs=[VMEM] * 5,
        out_shape=[
            struct((side * BLOCK, out_width), F32),
            struct((count, half), F32),
            struct((count, wake), F32),
            struct((BLOCK, out_width), F32),
            struct((BLOCK, out_width), F32),
        ],
        compiler_params=params(),
        cost_estimate=cost(count * half * width, half * width),
        name="adjoint_two_give",
    )(
        scalars, start, target, self_half, upper, lower, held,
        *parts,
    )
    induced = cols_parts(induced)
    give, *induced = lax.optimization_barrier((give, *induced))
    give = swap(give)
    image, image_rounded, bases_mine, bases_send = pl.pallas_call(
        functools.partial(image_kernel, len(induced)),
        in_specs=[SMEM] + [VMEM] * (2 + len(induced)),
        out_specs=[VMEM] * 4,
        out_shape=[
            struct((count, half), F32),
            struct((count, half), BF16),
            struct((count, out_width), F32),
            struct((count, out_width), F32),
        ],
        compiler_params=params(4),
        name="image",
    )(scalars, right_half, self_half, *induced)
    shards = [lax.ppermute(image_rounded, GRID, fetch(j)) for j in range(2)]
    keep = pl.pallas_call(
        functools.partial(adjoint_keep_kernel, tile),
        in_specs=[SMEM] + [VMEM] * 5 + [ANY],
        out_specs=VMEM,
        out_shape=struct((side * BLOCK, out_width), F32),
        compiler_params=params(),
        cost_estimate=cost(count * half * width, half * width),
        name="adjoint_two_keep",
    )(scalars, adjoint, carried, upper, lower, held, image_rounded)

    keep, *shards = lax.optimization_barrier((keep, *shards))
    shards = shards + [swap(value) for value in shards]
    induced = forward(tuple(CHUNKS + i for i in range(4)), shards, False, "forward_two")

    totals = pl.pallas_call(
        collect_kernel,
        in_specs=[SMEM, VMEM, VMEM, ANY],
        out_specs=[VMEM] * side,
        out_shape=[struct((BLOCK, out_width), F32)] * side,
        compiler_params=params(4),
        name="collect",
    )(scalars, keep, give, induced)

    induced = cols_parts(induced)
    system_keep, system_give = pl.pallas_call(
        functools.partial(system_kernel, len(induced)),
        in_specs=[SMEM] + [VMEM] * (3 + len(induced)),
        out_specs=[VMEM] * 2,
        out_shape=[struct((count, LANES), F32)] * 2,
        compiler_params=params(4),
        name="system",
    )(scalars, right_half, image, self_half, *induced)
    system = system_keep + swap(system_give)
    systems = [system] + [lax.ppermute(system, "rows", flip(k, n_rows)) for k in range(1, n_rows)]
    solution = pl.pallas_call(
        functools.partial(solve_kernel, len(systems)),
        in_specs=[SMEM] + [VMEM] * (2 + len(systems)),
        out_specs=VMEM,
        out_shape=struct((BLOCK, out_width), F32),
        compiler_params=params(4),
        name="solve",
    )(scalars, bases_mine, swap(bases_send), *systems)

    totals = [lax.ppermute(totals[k], GRID, cross(k)) for k in range(side)]
    adjoint = pl.pallas_call(
        functools.partial(update_kernel, len(totals)),
        in_specs=[SMEM] + [VMEM] * (4 + len(totals)),
        out_specs=VMEM,
        out_shape=struct((BLOCK, out_width), F32),
        compiler_params=params(4),
        name="update",
    )(scalars, adjoint_mine, swap(adjoint_send), self_row, objectives, *totals)
    return (solution, adjoint)


def solution(mesh):
    in_specs = (
        P(("groups", "rows"), "cols"),
        P(("groups", "rows"), "cols"),
        P(("groups", "rows")),
        P(("groups", "cols")),
        P(("groups", "cols")),
        P(("groups", "rows")),
        P(None, "rows"),
        P(None, "rhs"),
        P("rhs"),
        P("rhs", "rows"),
    )
    out_specs = (P("rhs", ("groups", "rows", "cols")), P("rhs", ("groups", "rows", "cols")))
    return jax.shard_map(
        per_device, mesh=mesh, in_specs=in_specs, out_specs=out_specs, check_vma=False
    )
```

```python
import functools

import jax
import jax.numpy as jnp
from jax import lax
from jax.experimental import pallas as pl
from jax.experimental.pallas import tpu as pltpu
from jax.sharding import PartitionSpec as P

BLOCK = 8
LANES = 128
SHIFT = 3.0
GRID = ("rows", "cols", "rhs")
F32 = jnp.float32
BF16 = jnp.bfloat16

VMEM = pl.BlockSpec(memory_space=pltpu.VMEM)
SMEM = pl.BlockSpec(memory_space=pltpu.SMEM)
ANY = pl.BlockSpec(memory_space=pl.ANY)

CORE, COLUMNS, ROW, BEGIN, HOLDER, SPAN, CHUNKS = range(7)


def dot(left, right, dims):
    return lax.dot_general(left, right, (dims, ((), ())), preferred_element_type=F32)


def precise(left, right, dims):
    return lax.dot_general(
        left, right, (dims, ((), ())), precision=lax.Precision.HIGHEST, preferred_element_type=F32
    )


def low_onehot(index):
    low = jnp.bitwise_and(index, LANES - 1)
    hit = lax.broadcasted_iota(jnp.int32, (LANES, index.shape[1]), 0) == low
    return jnp.where(hit, 1.0, 0.0).astype(BF16)


def take_columns(field, index):
    rows, width = field.shape
    chunks = width // LANES
    stacked = jnp.concatenate(
        [field[:, i * LANES : (i + 1) * LANES] for i in range(chunks)], axis=0
    )
    picked = dot(stacked, low_onehot(index), ((1,), (0,)))
    high = jnp.right_shift(index, 7)
    total = jnp.zeros((rows, index.shape[1]), F32)
    for i in range(chunks):
        total = total + jnp.where(high == i, picked[i * rows : (i + 1) * rows], 0.0)
    return total


def put_columns(values, index, width):
    rows = values.shape[0]
    chunks = width // LANES
    high = jnp.right_shift(index, 7)
    stacked = jnp.concatenate(
        [jnp.where(high == i, values, 0.0).astype(BF16) for i in range(chunks)], axis=0
    )
    spread = dot(stacked, low_onehot(index), ((1,), (1,)))
    return jnp.concatenate([spread[i * rows : (i + 1) * rows] for i in range(chunks)], axis=1)


def both_cores(core, own, other):
    first = jnp.where(core == 0, own, other)
    second = jnp.where(core == 0, other, own)
    return jnp.concatenate([first, second], axis=0)


def load_copies(influence, wake, held, sems, first, chunk):
    def copies(i):
        source = pl.ds(pl.multiple_of(first + i * chunk, 16), chunk)
        target = pl.ds(i * chunk, chunk)
        panels = influence.shape[1]
        return (
            pltpu.make_async_copy(
                influence.at[source], held.at[target, pl.ds(0, panels)], sems.at[0, i]
            ),
            pltpu.make_async_copy(
                wake.at[source], held.at[target, pl.ds(panels, wake.shape[1])], sems.at[1, i]
            ),
        )

    return copies


def right_kernel(
    half, scalars, pitch, pitch_other, modes, modes_other, blade, shapes, right, right_half
):
    core = scalars[CORE]
    blades = pitch.shape[0]
    blade_onehot = jnp.where(
        lax.broadcasted_iota(jnp.int32, (blades, blade.shape[1]), 0) == blade[...], 1.0, 0.0
    )
    for b in range(2):
        own = core == b
        amount = jnp.where(own, pitch[...], pitch_other[...])
        mode = jnp.where(own, modes[...], modes_other[...])
        mode_onehot = jnp.where(
            lax.broadcasted_iota(jnp.int32, (shapes.shape[0], BLOCK), 0) == mode, 1.0, 0.0
        )
        pattern = precise(mode_onehot, shapes[...], ((0,), (0,)))
        factor = precise(amount, blade_onehot, ((0,), (0,)))
        right[b * BLOCK : (b + 1) * BLOCK, :] = pattern * factor
    right_half[...] = right[:, pl.ds(pl.multiple_of(core * half, LANES), half)]


def local_wake(scalars, upper, lower):
    start = scalars[COLUMNS]
    return upper[...] - start, lower[...] - start


def load_adjoint_kernel(
    chunk, scalars, objectives, objectives_other, self_term, upper, lower, influence, wake,
    keep, give, start, target, self_half, held, whole, sems
):
    half = start.shape[1]
    piece = keep.shape[1]
    panels = 2 * piece
    core = scalars[CORE]
    copies = load_copies(influence, wake, held, sems, core * half, chunk)
    steps = held.shape[0] // chunk
    for i in range(steps):
        for copy in copies(i):
            copy.start()
    span = pl.ds(pl.multiple_of(core * half, LANES), half)
    target[...] = both_cores(core, objectives[:, span], objectives_other[:, span])
    self_half[...] = self_term[:, span]
    start[...] = target[...] / self_half[...]
    for i in range(steps):
        for copy in copies(i):
            copy.wait()
        rows = slice(i * chunk, (i + 1) * chunk)
        part = dot(start[:, rows].astype(BF16), held[rows, :], ((1,), (0,)))
        if i == 0:
            whole[...] = part
        else:
            whole[...] += part
    upper_local, lower_local = local_wake(scalars, upper, lower)
    carried = whole[:, panels:]
    whole[:, 0:panels] += put_columns(carried, upper_local, panels) - put_columns(
        carried, lower_local, panels
    )
    keep[...] = whole[:, pl.ds(pl.multiple_of(core * piece, LANES), piece)]
    give[...] = whole[:, pl.ds(pl.multiple_of((1 - core) * piece, LANES), piece)]


def adjoint_piece(tile, scalars, field, which, carried, upper, lower, held, out):
    width = out.shape[1]
    piece = out.shape[0] // (2 * BLOCK) * width
    begin = which * piece
    upper_local, lower_local = local_wake(scalars, upper, lower)
    spread = put_columns(carried, upper_local - begin, piece) - put_columns(
        carried, lower_local - begin, piece
    )
    for start in range(0, piece, tile):
        span = pl.ds(pl.multiple_of(begin + start, LANES), tile)
        part = (
            dot(field, held[:, span], ((1,), (0,)))
            + spread[:, start : start + tile]
        )
        col, offset = divmod(start, width)
        for b in range(2):
            goal = (col * 2 + b) * BLOCK
            out[goal : goal + BLOCK, offset : offset + tile] = part[b * BLOCK : (b + 1) * BLOCK]


def adjoint_give_kernel(
    tile, n_in, scalars, previous, target, self_half, upper, lower, held, *rest
):
    parts, (give, adjoint, carried, mine, send) = rest[:n_in], rest[n_in:]
    image = self_half[...] * previous[...]
    for part in parts:
        image = image + part[...].astype(F32)
    adjoint[...] = previous[...] + (target[...] - image) / self_half[...]
    to_output(scalars, (adjoint,), mine, send)
    field = adjoint[...].astype(BF16)
    panels = held.shape[1] - carried.shape[1]
    carried[...] = dot(field, held[:, panels:], ((1,), (0,)))
    which = 1 - scalars[CORE]
    adjoint_piece(
        tile, scalars, field, which, carried[...], upper, lower, held, give
    )


def adjoint_keep_kernel(
    tile, scalars, adjoint, carried, upper, lower, held, ready, keep
):
    field = adjoint[...].astype(BF16)
    which = scalars[CORE]
    adjoint_piece(
        tile, scalars, field, which, carried[...], upper, lower, held, keep
    )


def forward_kernel(tile, places, split, scalars, upper, lower, held, *rest):
    shards, (out, field) = rest[: len(places)], rest[len(places) :]
    count = out.shape[0]
    for place, ref in zip(places, shards):
        span = pl.ds(pl.multiple_of(scalars[place], LANES), ref.shape[1])
        if split:
            high = ref[...].astype(BF16)
            field[0:count, span] = high
            field[count:, span] = (ref[...] - high.astype(F32)).astype(BF16)
        else:
            field[:, span] = ref[...]
    panels = held.shape[1] - upper.shape[1]
    source = field[:, 0:panels]
    upper_local, lower_local = local_wake(scalars, upper, lower)
    strength = take_columns(source, upper_local) - take_columns(source, lower_local)
    if split:
        strength = strength[0:count] + strength[count:]
        high = strength.astype(BF16)
        field[0:count, panels:] = high
        field[count:, panels:] = (strength - high.astype(F32)).astype(BF16)
    else:
        field[:, panels:] = strength.astype(BF16)
    for start in range(0, held.shape[0], tile):
        result = dot(field[...], held[start : start + tile, :], ((1,), (1,)))
        if split:
            result = result[0:count] + result[count:]
        out[:, start : start + tile] = result


def system_kernel(n_parts, scalars, basis, image, self_half, *rest):
    parts, (keep, give) = rest[:n_parts], rest[n_parts:]
    second = self_half[...] * image[...]
    for part in parts:
        second = second + part[...]
    first = image[...] + SHIFT * basis[...]
    core = scalars[CORE]
    keep[...] = jnp.zeros_like(keep)
    give[...] = jnp.zeros_like(give)
    for b in range(2):
        rows = slice(b * BLOCK, (b + 1) * BLOCK)
        images = jnp.concatenate([first[rows], second[rows]], axis=0)
        full = jnp.concatenate([images, basis[rows, :]], axis=0)
        system = precise(images, full, ((1,), (1,)))
        size = system.shape[1]

        @pl.when(core == b)
        def _():
            keep[:, 0:size] = system

        @pl.when(core != b)
        def _():
            give[:, 0:size] = system


def to_output(scalars, values, mine, send):
    width = mine.shape[1]
    core = scalars[CORE]
    span = pl.ds(pl.multiple_of(scalars[BEGIN], LANES), width)
    for i, value in enumerate(values):
        first = value[0:BLOCK, span]
        second = value[BLOCK : 2 * BLOCK, span]
        rows = slice(i * BLOCK, (i + 1) * BLOCK)
        mine[rows, :] = jnp.where(core == 0, first, second)
        send[rows, :] = jnp.where(core == 0, second, first)


def combine_kernel(scalars, keep, other, first, second):
    half = first.shape[1]
    low = (keep[:, 0:half] + other[:, 0:half]).astype(BF16)
    high = (keep[:, half:] + other[:, half:]).astype(BF16)
    odd = scalars[ROW] % 2 == 1
    first[...] = jnp.where(odd, high, low)
    second[...] = jnp.where(odd, low, high)


def image_kernel(n_parts, scalars, right_half, self_half, *rest):
    parts, (image, rounded, mine, send) = rest[:n_parts], rest[n_parts:]
    total = (self_half[...] - SHIFT) * right_half[...]
    for part in parts:
        total = total + part[...]
    image[...] = total
    rounded[...] = total.astype(BF16)
    to_output(scalars, (right_half, image), mine, send)


def collect_kernel(scalars, keep, other, *outs):
    for k, out in enumerate(outs):
        rows = pl.ds(pl.multiple_of(jnp.bitwise_xor(scalars[ROW], k) * BLOCK, BLOCK), BLOCK)
        out[...] = keep[rows, :] + other[rows, :]


def update_kernel(n_parts, scalars, mine, received, self_term, objectives, *rest):
    parts, out = rest[:n_parts], rest[n_parts]
    span = pl.ds(pl.multiple_of(scalars[SPAN], LANES), out.shape[1])
    previous = jnp.where(scalars[HOLDER] == 1, mine[...], received[...])
    scale = self_term[:, span]
    image = scale * previous
    for part in parts:
        image = image + part[...]
    out[...] = previous + (objectives[:, span] - image) / scale


def solve_kernel(n_parts, scalars, mine, received, *rest):
    parts, out = rest[:n_parts], rest[n_parts]
    basis = jnp.where(scalars[HOLDER] == 1, mine[...], received[...])
    system = parts[0][...]
    for part in parts[1:]:
        system = system + part[...]
    size = basis.shape[0]
    row = lax.broadcasted_iota(jnp.int32, (size, 1), 0)
    for j in range(size):
        pivot_row = system[j : j + 1, :] / system[j : j + 1, j : j + 1]
        factor = jnp.where(row == j, 0.0, system[:, j : j + 1])
        system = jnp.where(row == j, pivot_row, system - factor * pivot_row)
    weights = system[:, size : size + BLOCK]
    out[...] = precise(weights, basis, ((0,), (0,)))


def argument(value):
    return pltpu.with_memory_space_constraint(value, pltpu.HBM)


def keep_in_vmem(value):
    return pltpu.with_memory_space_constraint(value, pltpu.VMEM)


def params(mib=20):
    return pltpu.CompilerParams(vmem_limit_bytes=mib << 20)


def cost(flops, size):
    return pl.CostEstimate(flops=flops, bytes_accessed=size, transcendentals=0)


def per_device(
    influence,
    wake_influence,
    self_term,
    wake_upper,
    wake_lower,
    blade_of,
    mode_shapes,
    blade_pitch,
    design_map,
    objectives,
):
    influence = argument(influence)
    wake_influence = argument(wake_influence)
    n_rows, n_cols, n_rhs = (lax.axis_size(name) for name in GRID)
    side = n_cols * n_rhs
    piece, panels = influence.shape
    wake = wake_influence.shape[1]
    half = piece // n_rhs
    out_width = piece // n_cols
    count = 2 * BLOCK
    width = panels + wake
    if n_rows != side or n_rhs != 2 or panels != 2 * piece:
        raise ValueError("unsupported mesh")
    row_index = lax.axis_index("rows")
    col_index = lax.axis_index("cols")
    core = lax.axis_index("rhs")

    def cross(k):
        return [(a * side + b, b * side + (a ^ k)) for a in range(side) for b in range(side)]

    def fetch(j):
        return [
            (a * side + c * n_rhs + h, ((h ^ j) * n_cols + c) * side + a)
            for a in range(side)
            for c in range(n_cols)
            for h in range(n_rhs)
        ]

    def flip(k, size):
        return [(i, i ^ k) for i in range(size)]

    def swap(value):
        return lax.ppermute(value, "rhs", flip(1, 2))

    def cols_parts(value):
        return [value] + [lax.ppermute(value, "cols", flip(k, n_cols)) for k in range(1, n_cols)]

    near = core * piece
    far = (1 - core) * piece
    chunk_half = row_index // n_cols
    places = [
        near + chunk_half * half,
        near + (1 - chunk_half) * half,
        far + chunk_half * half,
        far + (1 - chunk_half) * half,
        near,
        far,
    ]
    span = col_index * out_width
    holder = (core == span // half).astype(jnp.int32)
    scalars = jnp.stack(
        [core, col_index * panels, row_index, span % half, holder, span] + places
    ).astype(jnp.int32)
    self_row = argument(self_term[None, :])
    objectives = argument(objectives)
    upper = argument(wake_upper[None, :])
    lower = argument(wake_lower[None, :])

    chunk = half // 8
    struct = jax.ShapeDtypeStruct

    modes = design_map[None, :]
    objectives_other = swap(objectives)
    right, right_half = pl.pallas_call(
        functools.partial(right_kernel, half),
        in_specs=[SMEM] + [VMEM] * 6,
        out_specs=[VMEM] * 2,
        out_shape=[struct((count, piece), F32), struct((count, half), F32)],
        compiler_params=params(4),
        name="right",
    )(
        scalars, argument(blade_pitch), (swap(blade_pitch)), argument(modes),
        (swap(modes)),
        argument(blade_of[None, :]), argument(mode_shapes),
    )
    right, objectives_other = lax.optimization_barrier((right, objectives_other))
    right_near = lax.ppermute(right, GRID, cross(0))

    keep, give, start, target, self_half, held = pl.pallas_call(
        functools.partial(load_adjoint_kernel, chunk),
        in_specs=[SMEM] + [VMEM] * 5 + [ANY, ANY],
        out_specs=[VMEM] * 6,
        out_shape=[
            struct((count, piece), F32),
            struct((count, piece), F32),
            struct((count, half), F32),
            struct((count, half), F32),
            struct((1, half), F32),
            pltpu.VMEM((half, width), BF16),
        ],
        scratch_shapes=[
            pltpu.VMEM((count, width), F32),
            pltpu.SemaphoreType.DMA((2, half // chunk)),
        ],
        compiler_params=params(),
        cost_estimate=cost(2 * count * half * width, 2 * half * width),
        name="adjoint_one",
    )(
        scalars, objectives, objectives_other, self_row, upper, lower, influence, wake_influence
    )
    right_near, start = lax.optimization_barrier((right_near, start))
    right_far = swap(right_near)
    held = keep_in_vmem(held)

    def forward(places, shards, split, name):
        rows = 2 * count if split else count
        return pl.pallas_call(
            functools.partial(forward_kernel, 512, places, split),
            in_specs=[SMEM] + [VMEM] * (3 + len(shards)),
            out_specs=VMEM,
            out_shape=struct((count, half), F32),
            scratch_shapes=[pltpu.VMEM((rows, width), BF16)],
            compiler_params=params(),
            cost_estimate=cost(2 * count * half * width, 2 * half * width),
            name=name,
        )(scalars, upper, lower, held, *shards)

    sends = pl.pallas_call(
        combine_kernel,
        in_specs=[SMEM] + [VMEM] * 2,
        out_specs=[VMEM] * 2,
        out_shape=[struct((count, half), BF16)] * 2,
        compiler_params=params(4),
        name="combine",
    )(scalars, keep, swap(give))

    right_far, *sends = lax.optimization_barrier((right_far, *sends))
    induced = forward(
        (CHUNKS + 4, CHUNKS + 5), [right_near, right_far], True, "forward_one"
    )
    parts = [lax.ppermute(sends[k % 2], GRID, cross(k)) for k in range(side)]
    induced, *parts = lax.optimization_barrier((induced, *parts))

    tile = min(512, out_width)
    give, adjoint, carried, adjoint_mine, adjoint_send = pl.pallas_call(
        functools.partial(adjoint_give_kernel, tile, len(parts)),
        in_specs=[SMEM] + [VMEM] * (6 + len(parts)),
        out_specs=[VMEM] * 5,
        out_shape=[
            struct((side * BLOCK, out_width), F32),
            struct((count, half), F32),
            struct((count, wake), F32),
            struct((BLOCK, out_width), F32),
            struct((BLOCK, out_width), F32),
        ],
        compiler_params=params(),
        cost_estimate=cost(count * half * width, half * width),
        name="adjoint_two_give",
    )(
        scalars, start, target, self_half, upper, lower, held,
        *parts,
    )
    induced = cols_parts(induced)
    give, *induced = lax.optimization_barrier((give, *induced))
    give = swap(give)
    image, image_rounded, bases_mine, bases_send = pl.pallas_call(
        functools.partial(image_kernel, len(induced)),
        in_specs=[SMEM] + [VMEM] * (2 + len(induced)),
        out_specs=[VMEM] * 4,
        out_shape=[
            struct((count, half), F32),
            struct((count, half), BF16),
            struct((count, out_width), F32),
            struct((count, out_width), F32),
        ],
        compiler_params=params(4),
        name="image",
    )(scalars, right_half, self_half, *induced)
    shards = [lax.ppermute(image_rounded, GRID, fetch(j)) for j in range(2)]
    keep = pl.pallas_call(
        functools.partial(adjoint_keep_kernel, tile),
        in_specs=[SMEM] + [VMEM] * 5 + [ANY],
        out_specs=VMEM,
        out_shape=struct((side * BLOCK, out_width), F32),
        compiler_params=params(),
        cost_estimate=cost(count * half * width, half * width),
        name="adjoint_two_keep",
    )(scalars, adjoint, carried, upper, lower, held, image_rounded)

    keep, *shards = lax.optimization_barrier((keep, *shards))
    shards = shards + [swap(value) for value in shards]
    totals = pl.pallas_call(
        collect_kernel,
        in_specs=[SMEM, VMEM, VMEM],
        out_specs=[VMEM] * side,
        out_shape=[struct((BLOCK, out_width), F32)] * side,
        compiler_params=params(4),
        name="collect",
    )(scalars, keep, give)
    *shards, first_total = lax.optimization_barrier((*shards, totals[0]))
    totals = [first_total, *totals[1:]]
    induced = forward(tuple(CHUNKS + i for i in range(4)), shards, False, "forward_two")

    induced, *totals = lax.optimization_barrier((induced, *totals))
    totals = [lax.ppermute(totals[k], GRID, cross(k)) for k in range(side)]

    induced = cols_parts(induced)
    system_keep, system_give = pl.pallas_call(
        functools.partial(system_kernel, len(induced)),
        in_specs=[SMEM] + [VMEM] * (3 + len(induced)),
        out_specs=[VMEM] * 2,
        out_shape=[struct((count, LANES), F32)] * 2,
        compiler_params=params(4),
        name="system",
    )(scalars, right_half, image, self_half, *induced)
    system_give, *totals = lax.optimization_barrier((system_give, *totals))
    system = system_keep + swap(system_give)
    systems = [system] + [lax.ppermute(system, "rows", flip(k, n_rows)) for k in range(1, n_rows)]
    solution = pl.pallas_call(
        functools.partial(solve_kernel, len(systems)),
        in_specs=[SMEM] + [VMEM] * (2 + len(systems)),
        out_specs=VMEM,
        out_shape=struct((BLOCK, out_width), F32),
        compiler_params=params(4),
        name="solve",
    )(scalars, bases_mine, swap(bases_send), *systems)

    adjoint = pl.pallas_call(
        functools.partial(update_kernel, len(totals)),
        in_specs=[SMEM] + [VMEM] * (4 + len(totals)),
        out_specs=VMEM,
        out_shape=struct((BLOCK, out_width), F32),
        compiler_params=params(4),
        name="update",
    )(scalars, adjoint_mine, swap(adjoint_send), self_row, objectives, *totals)
    return (solution, adjoint)


def solution(mesh):
    in_specs = (
        P(("groups", "rows"), "cols"),
        P(("groups", "rows"), "cols"),
        P(("groups", "rows")),
        P(("groups", "cols")),
        P(("groups", "cols")),
        P(("groups", "rows")),
        P(None, "rows"),
        P(None, "rhs"),
        P("rhs"),
        P("rhs", "rows"),
    )
    out_specs = (P("rhs", ("groups", "rows", "cols")), P("rhs", ("groups", "rows", "cols")))
    return jax.shard_map(
        per_device, mesh=mesh, in_specs=in_specs, out_specs=out_specs, check_vma=False
    )
```

```python
import functools

import jax
import jax.numpy as jnp
from jax import lax
from jax.experimental import pallas as pl
from jax.experimental.pallas import tpu as pltpu
from jax.sharding import PartitionSpec as P

BLOCK = 8
LANES = 128
SHIFT = 3.0
GRID = ("rows", "cols", "rhs")
F32 = jnp.float32
BF16 = jnp.bfloat16

VMEM = pl.BlockSpec(memory_space=pltpu.VMEM)
SMEM = pl.BlockSpec(memory_space=pltpu.SMEM)
ANY = pl.BlockSpec(memory_space=pl.ANY)

CORE, COLUMNS, ROW, BEGIN, HOLDER, SPAN, CHUNKS = range(7)


def dot(left, right, dims):
    return lax.dot_general(left, right, (dims, ((), ())), preferred_element_type=F32)


def precise(left, right, dims):
    return lax.dot_general(
        left, right, (dims, ((), ())), precision=lax.Precision.HIGHEST, preferred_element_type=F32
    )


def low_onehot(index):
    low = jnp.bitwise_and(index, LANES - 1)
    hit = lax.broadcasted_iota(jnp.int32, (LANES, index.shape[1]), 0) == low
    return jnp.where(hit, 1.0, 0.0).astype(BF16)


def take_columns(field, index):
    rows, width = field.shape
    chunks = width // LANES
    stacked = jnp.concatenate(
        [field[:, i * LANES : (i + 1) * LANES] for i in range(chunks)], axis=0
    )
    picked = dot(stacked, low_onehot(index), ((1,), (0,)))
    high = jnp.right_shift(index, 7)
    total = jnp.zeros((rows, index.shape[1]), F32)
    for i in range(chunks):
        total = total + jnp.where(high == i, picked[i * rows : (i + 1) * rows], 0.0)
    return total


def put_columns(values, index, width):
    rows = values.shape[0]
    chunks = width // LANES
    high = jnp.right_shift(index, 7)
    stacked = jnp.concatenate(
        [jnp.where(high == i, values, 0.0).astype(BF16) for i in range(chunks)], axis=0
    )
    spread = dot(stacked, low_onehot(index), ((1,), (1,)))
    return jnp.concatenate([spread[i * rows : (i + 1) * rows] for i in range(chunks)], axis=1)


def both_cores(core, own, other):
    first = jnp.where(core == 0, own, other)
    second = jnp.where(core == 0, other, own)
    return jnp.concatenate([first, second], axis=0)


def load_copies(influence, wake, held, sems, first, chunk):
    def copies(i):
        source = pl.ds(pl.multiple_of(first + i * chunk, 16), chunk)
        target = pl.ds(i * chunk, chunk)
        panels = influence.shape[1]
        return (
            pltpu.make_async_copy(
                influence.at[source], held.at[target, pl.ds(0, panels)], sems.at[0, i]
            ),
            pltpu.make_async_copy(
                wake.at[source], held.at[target, pl.ds(panels, wake.shape[1])], sems.at[1, i]
            ),
        )

    return copies


def right_kernel(
    half, scalars, pitch, pitch_other, modes, modes_other, blade, shapes, right, right_half
):
    core = scalars[CORE]
    blades = pitch.shape[0]
    blade_onehot = jnp.where(
        lax.broadcasted_iota(jnp.int32, (blades, blade.shape[1]), 0) == blade[...], 1.0, 0.0
    )
    for b in range(2):
        own = core == b
        amount = jnp.where(own, pitch[...], pitch_other[...])
        mode = jnp.where(own, modes[...], modes_other[...])
        mode_onehot = jnp.where(
            lax.broadcasted_iota(jnp.int32, (shapes.shape[0], BLOCK), 0) == mode, 1.0, 0.0
        )
        pattern = precise(mode_onehot, shapes[...], ((0,), (0,)))
        factor = precise(amount, blade_onehot, ((0,), (0,)))
        right[b * BLOCK : (b + 1) * BLOCK, :] = pattern * factor
    right_half[...] = right[:, pl.ds(pl.multiple_of(core * half, LANES), half)]


def local_wake(scalars, upper, lower):
    start = scalars[COLUMNS]
    return upper[...] - start, lower[...] - start


def load_adjoint_kernel(
    chunk, scalars, objectives, objectives_other, self_term, upper, lower, influence, wake,
    keep, give, start, target, self_half, held, whole, sems
):
    half = start.shape[1]
    piece = keep.shape[1]
    panels = 2 * piece
    core = scalars[CORE]
    copies = load_copies(influence, wake, held, sems, core * half, chunk)
    steps = held.shape[0] // chunk
    for i in range(steps):
        for copy in copies(i):
            copy.start()
    span = pl.ds(pl.multiple_of(core * half, LANES), half)
    target[...] = both_cores(core, objectives[:, span], objectives_other[:, span])
    self_half[...] = self_term[:, span]
    start[...] = target[...] / self_half[...]
    for i in range(steps):
        for copy in copies(i):
            copy.wait()
        rows = slice(i * chunk, (i + 1) * chunk)
        part = dot(start[:, rows].astype(BF16), held[rows, :], ((1,), (0,)))
        if i == 0:
            whole[...] = part
        else:
            whole[...] += part
    upper_local, lower_local = local_wake(scalars, upper, lower)
    carried = whole[:, panels:]
    whole[:, 0:panels] += put_columns(carried, upper_local, panels) - put_columns(
        carried, lower_local, panels
    )
    keep[...] = whole[:, pl.ds(pl.multiple_of(core * piece, LANES), piece)]
    give[...] = whole[:, pl.ds(pl.multiple_of((1 - core) * piece, LANES), piece)]


def adjoint_piece(tile, scalars, field, which, carried, upper, lower, held, out):
    width = out.shape[1]
    piece = out.shape[0] // (2 * BLOCK) * width
    begin = which * piece
    upper_local, lower_local = local_wake(scalars, upper, lower)
    spread = put_columns(carried, upper_local - begin, piece) - put_columns(
        carried, lower_local - begin, piece
    )
    for start in range(0, piece, tile):
        span = pl.ds(pl.multiple_of(begin + start, LANES), tile)
        part = (
            dot(field, held[:, span], ((1,), (0,)))
            + spread[:, start : start + tile]
        )
        col, offset = divmod(start, width)
        for b in range(2):
            goal = (col * 2 + b) * BLOCK
            out[goal : goal + BLOCK, offset : offset + tile] = part[b * BLOCK : (b + 1) * BLOCK]


def adjoint_give_kernel(
    tile, n_in, scalars, previous, target, self_half, upper, lower, held, *rest
):
    parts, (give, adjoint, carried, mine, send) = rest[:n_in], rest[n_in:]
    image = self_half[...] * previous[...]
    for part in parts:
        image = image + part[...].astype(F32)
    adjoint[...] = previous[...] + (target[...] - image) / self_half[...]
    to_output(scalars, (adjoint,), mine, send)
    field = adjoint[...].astype(BF16)
    panels = held.shape[1] - carried.shape[1]
    carried[...] = dot(field, held[:, panels:], ((1,), (0,)))
    which = 1 - scalars[CORE]
    adjoint_piece(
        tile, scalars, field, which, carried[...], upper, lower, held, give
    )


def adjoint_keep_kernel(
    tile, scalars, adjoint, carried, upper, lower, held, ready, keep
):
    field = adjoint[...].astype(BF16)
    which = scalars[CORE]
    adjoint_piece(
        tile, scalars, field, which, carried[...], upper, lower, held, keep
    )


def forward_kernel(tile, places, split, scalars, upper, lower, held, *rest):
    shards, (out, field) = rest[: len(places)], rest[len(places) :]
    count = out.shape[0]
    for place, ref in zip(places, shards):
        span = pl.ds(pl.multiple_of(scalars[place], LANES), ref.shape[1])
        if split:
            high = ref[...].astype(BF16)
            field[0:count, span] = high
            field[count:, span] = (ref[...] - high.astype(F32)).astype(BF16)
        else:
            field[:, span] = ref[...]
    panels = held.shape[1] - upper.shape[1]
    source = field[:, 0:panels]
    upper_local, lower_local = local_wake(scalars, upper, lower)
    strength = take_columns(source, upper_local) - take_columns(source, lower_local)
    if split:
        strength = strength[0:count] + strength[count:]
        high = strength.astype(BF16)
        field[0:count, panels:] = high
        field[count:, panels:] = (strength - high.astype(F32)).astype(BF16)
    else:
        field[:, panels:] = strength.astype(BF16)
    for start in range(0, held.shape[0], tile):
        result = dot(field[...], held[start : start + tile, :], ((1,), (1,)))
        if split:
            result = result[0:count] + result[count:]
        out[:, start : start + tile] = result


def system_kernel(n_parts, scalars, basis, image, self_half, *rest):
    parts, (keep, give) = rest[:n_parts], rest[n_parts:]
    second = self_half[...] * image[...]
    for part in parts:
        second = second + part[...]
    first = image[...] + SHIFT * basis[...]
    core = scalars[CORE]
    keep[...] = jnp.zeros_like(keep)
    give[...] = jnp.zeros_like(give)
    for b in range(2):
        rows = slice(b * BLOCK, (b + 1) * BLOCK)
        images = jnp.concatenate([first[rows], second[rows]], axis=0)
        full = jnp.concatenate([images, basis[rows, :]], axis=0)
        system = precise(images, full, ((1,), (1,)))
        size = system.shape[1]

        @pl.when(core == b)
        def _():
            keep[:, 0:size] = system

        @pl.when(core != b)
        def _():
            give[:, 0:size] = system


def to_output(scalars, values, mine, send):
    width = mine.shape[1]
    core = scalars[CORE]
    span = pl.ds(pl.multiple_of(scalars[BEGIN], LANES), width)
    for i, value in enumerate(values):
        first = value[0:BLOCK, span]
        second = value[BLOCK : 2 * BLOCK, span]
        rows = slice(i * BLOCK, (i + 1) * BLOCK)
        mine[rows, :] = jnp.where(core == 0, first, second)
        send[rows, :] = jnp.where(core == 0, second, first)


def combine_kernel(scalars, keep, other, first, second):
    half = first.shape[1]
    low = (keep[:, 0:half] + other[:, 0:half]).astype(BF16)
    high = (keep[:, half:] + other[:, half:]).astype(BF16)
    odd = scalars[ROW] % 2 == 1
    first[...] = jnp.where(odd, high, low)
    second[...] = jnp.where(odd, low, high)


def image_kernel(n_parts, scalars, right_half, self_half, *rest):
    parts, (image, rounded, mine, send) = rest[:n_parts], rest[n_parts:]
    total = (self_half[...] - SHIFT) * right_half[...]
    for part in parts:
        total = total + part[...]
    image[...] = total
    rounded[...] = total.astype(BF16)
    to_output(scalars, (right_half, image), mine, send)


def collect_kernel(scalars, keep, other, *outs):
    for k, out in enumerate(outs):
        rows = pl.ds(pl.multiple_of(jnp.bitwise_xor(scalars[ROW], k) * BLOCK, BLOCK), BLOCK)
        out[...] = keep[rows, :] + other[rows, :]


def update_kernel(n_parts, scalars, mine, received, self_term, objectives, *rest):
    parts, out = rest[:n_parts], rest[n_parts]
    span = pl.ds(pl.multiple_of(scalars[SPAN], LANES), out.shape[1])
    previous = jnp.where(scalars[HOLDER] == 1, mine[...], received[...])
    scale = self_term[:, span]
    image = scale * previous
    for part in parts:
        image = image + part[...]
    out[...] = previous + (objectives[:, span] - image) / scale


def solve_kernel(n_parts, scalars, mine, received, *rest):
    parts, out = rest[:n_parts], rest[n_parts]
    basis = jnp.where(scalars[HOLDER] == 1, mine[...], received[...])
    system = parts[0][...]
    for part in parts[1:]:
        system = system + part[...]
    size = basis.shape[0]
    row = lax.broadcasted_iota(jnp.int32, (size, 1), 0)
    for j in range(size):
        pivot_row = system[j : j + 1, :] / system[j : j + 1, j : j + 1]
        factor = jnp.where(row == j, 0.0, system[:, j : j + 1])
        system = jnp.where(row == j, pivot_row, system - factor * pivot_row)
    weights = system[:, size : size + BLOCK]
    out[...] = precise(weights, basis, ((0,), (0,)))


def argument(value):
    return pltpu.with_memory_space_constraint(value, pltpu.HBM)


def keep_in_vmem(value):
    return pltpu.with_memory_space_constraint(value, pltpu.VMEM)


def params(mib=20):
    return pltpu.CompilerParams(vmem_limit_bytes=mib << 20)


def cost(flops, size):
    return pl.CostEstimate(flops=flops, bytes_accessed=size, transcendentals=0)


def per_device(
    influence,
    wake_influence,
    self_term,
    wake_upper,
    wake_lower,
    blade_of,
    mode_shapes,
    blade_pitch,
    design_map,
    objectives,
):
    influence = argument(influence)
    wake_influence = argument(wake_influence)
    n_rows, n_cols, n_rhs = (lax.axis_size(name) for name in GRID)
    side = n_cols * n_rhs
    piece, panels = influence.shape
    wake = wake_influence.shape[1]
    half = piece // n_rhs
    out_width = piece // n_cols
    count = 2 * BLOCK
    width = panels + wake
    if n_rows != side or n_rhs != 2 or panels != 2 * piece:
        raise ValueError("unsupported mesh")
    row_index = lax.axis_index("rows")
    col_index = lax.axis_index("cols")
    core = lax.axis_index("rhs")

    def cross(k):
        return [(a * side + b, b * side + (a ^ k)) for a in range(side) for b in range(side)]

    def fetch(j):
        return [
            (a * side + c * n_rhs + h, ((h ^ j) * n_cols + c) * side + a)
            for a in range(side)
            for c in range(n_cols)
            for h in range(n_rhs)
        ]

    def flip(k, size):
        return [(i, i ^ k) for i in range(size)]

    def swap(value):
        return lax.ppermute(value, "rhs", flip(1, 2))

    def cols_parts(value):
        return [value] + [lax.ppermute(value, "cols", flip(k, n_cols)) for k in range(1, n_cols)]

    near = core * piece
    far = (1 - core) * piece
    chunk_half = row_index // n_cols
    places = [
        near + chunk_half * half,
        near + (1 - chunk_half) * half,
        far + chunk_half * half,
        far + (1 - chunk_half) * half,
        near,
        far,
    ]
    span = col_index * out_width
    holder = (core == span // half).astype(jnp.int32)
    scalars = jnp.stack(
        [core, col_index * panels, row_index, span % half, holder, span] + places
    ).astype(jnp.int32)
    scalars = argument(scalars)
    self_row = argument(self_term[None, :])
    objectives = argument(objectives)
    upper = argument(wake_upper[None, :])
    lower = argument(wake_lower[None, :])

    chunk = half // 8
    struct = jax.ShapeDtypeStruct

    modes = design_map[None, :]
    objectives_other = swap(objectives)
    right, right_half = pl.pallas_call(
        functools.partial(right_kernel, half),
        in_specs=[SMEM] + [VMEM] * 6,
        out_specs=[VMEM] * 2,
        out_shape=[struct((count, piece), F32), struct((count, half), F32)],
        compiler_params=params(4),
        name="right",
    )(
        scalars, argument(blade_pitch), (swap(blade_pitch)), argument(modes),
        (swap(modes)),
        argument(blade_of[None, :]), argument(mode_shapes),
    )
    right, objectives_other = lax.optimization_barrier((right, objectives_other))
    right_near = lax.ppermute(right, GRID, cross(0))

    keep, give, start, target, self_half, held = pl.pallas_call(
        functools.partial(load_adjoint_kernel, chunk),
        in_specs=[SMEM] + [VMEM] * 5 + [ANY, ANY],
        out_specs=[VMEM] * 6,
        out_shape=[
            struct((count, piece), F32),
            struct((count, piece), F32),
            struct((count, half), F32),
            struct((count, half), F32),
            struct((1, half), F32),
            pltpu.VMEM((half, width), BF16),
        ],
        scratch_shapes=[
            pltpu.VMEM((count, width), F32),
            pltpu.SemaphoreType.DMA((2, half // chunk)),
        ],
        compiler_params=params(),
        cost_estimate=cost(2 * count * half * width, 2 * half * width),
        name="adjoint_one",
    )(
        scalars, objectives, argument(objectives_other), self_row, upper, lower, influence, wake_influence
    )
    right_near, start = lax.optimization_barrier((right_near, start))
    right_far = swap(right_near)
    held = keep_in_vmem(held)

    def forward(places, shards, split, name):
        rows = 2 * count if split else count
        return pl.pallas_call(
            functools.partial(forward_kernel, 512, places, split),
            in_specs=[SMEM] + [VMEM] * (3 + len(shards)),
            out_specs=VMEM,
            out_shape=struct((count, half), F32),
            scratch_shapes=[pltpu.VMEM((rows, width), BF16)],
            compiler_params=params(),
            cost_estimate=cost(2 * count * half * width, 2 * half * width),
            name=name,
        )(scalars, upper, lower, held, *map(keep_in_vmem, shards))

    sends = pl.pallas_call(
        combine_kernel,
        in_specs=[SMEM] + [VMEM] * 2,
        out_specs=[VMEM] * 2,
        out_shape=[struct((count, half), BF16)] * 2,
        compiler_params=params(4),
        name="combine",
    )(scalars, argument(keep), swap(give))

    right_far, *sends = lax.optimization_barrier((right_far, *sends))
    induced = forward(
        (CHUNKS + 4, CHUNKS + 5), [right_near, right_far], True, "forward_one"
    )
    parts = [lax.ppermute(sends[k % 2], GRID, cross(k)) for k in range(side)]
    induced, *parts = lax.optimization_barrier((induced, *parts))

    tile = min(512, out_width)
    give, adjoint, carried, adjoint_mine, adjoint_send = pl.pallas_call(
        functools.partial(adjoint_give_kernel, tile, len(parts)),
        in_specs=[SMEM] + [VMEM] * (6 + len(parts)),
        out_specs=[VMEM] * 5,
        out_shape=[
            struct((side * BLOCK, out_width), F32),
            struct((count, half), F32),
            struct((count, wake), F32),
            struct((BLOCK, out_width), F32),
            struct((BLOCK, out_width), F32),
        ],
        compiler_params=params(),
        cost_estimate=cost(count * half * width, half * width),
        name="adjoint_two_give",
    )(
        scalars, start, target, self_half, upper, lower, held,
        *map(keep_in_vmem, parts),
    )
    induced = cols_parts(induced)
    give, *induced = lax.optimization_barrier((give, *induced))
    give = swap(give)
    image, image_rounded, bases_mine, bases_send = pl.pallas_call(
        functools.partial(image_kernel, len(induced)),
        in_specs=[SMEM] + [VMEM] * (2 + len(induced)),
        out_specs=[VMEM] * 4,
        out_shape=[
            struct((count, half), F32),
            struct((count, half), BF16),
            struct((count, out_width), F32),
            struct((count, out_width), F32),
        ],
        compiler_params=params(4),
        name="image",
    )(scalars, right_half, self_half, *induced)
    shards = [lax.ppermute(image_rounded, GRID, fetch(j)) for j in range(2)]
    keep = pl.pallas_call(
        functools.partial(adjoint_keep_kernel, tile),
        in_specs=[SMEM] + [VMEM] * 5 + [ANY],
        out_specs=VMEM,
        out_shape=struct((side * BLOCK, out_width), F32),
        compiler_params=params(),
        cost_estimate=cost(count * half * width, half * width),
        name="adjoint_two_keep",
    )(scalars, adjoint, carried, upper, lower, held, keep_in_vmem(image_rounded))

    keep, *shards = lax.optimization_barrier((keep, *shards))
    shards = shards + [swap(value) for value in shards]
    totals = pl.pallas_call(
        collect_kernel,
        in_specs=[SMEM, VMEM, VMEM],
        out_specs=[VMEM] * side,
        out_shape=[struct((BLOCK, out_width), F32)] * side,
        compiler_params=params(4),
        name="collect",
    )(scalars, argument(keep), give)
    *shards, first_total = lax.optimization_barrier((*shards, totals[0]))
    totals = [first_total, *totals[1:]]
    induced = forward(tuple(CHUNKS + i for i in range(4)), shards, False, "forward_two")

    induced, *totals = lax.optimization_barrier((induced, *totals))
    totals = [lax.ppermute(totals[k], GRID, cross(k)) for k in range(side)]

    induced = cols_parts(induced)
    system_keep, system_give = pl.pallas_call(
        functools.partial(system_kernel, len(induced)),
        in_specs=[SMEM] + [VMEM] * (3 + len(induced)),
        out_specs=[VMEM] * 2,
        out_shape=[struct((count, LANES), F32)] * 2,
        compiler_params=params(4),
        name="system",
    )(scalars, right_half, image, self_half, *induced)
    system_give, *totals = lax.optimization_barrier((system_give, *totals))
    system = system_keep + swap(system_give)
    systems = [system] + [lax.ppermute(system, "rows", flip(k, n_rows)) for k in range(1, n_rows)]
    solution = pl.pallas_call(
        functools.partial(solve_kernel, len(systems)),
        in_specs=[SMEM] + [VMEM] * (2 + len(systems)),
        out_specs=VMEM,
        out_shape=struct((BLOCK, out_width), F32),
        compiler_params=params(4),
        name="solve",
    )(scalars, bases_mine, swap(bases_send), *systems)

    adjoint = pl.pallas_call(
        functools.partial(update_kernel, len(totals)),
        in_specs=[SMEM] + [VMEM] * (4 + len(totals)),
        out_specs=VMEM,
        out_shape=struct((BLOCK, out_width), F32),
        compiler_params=params(4),
        name="update",
    )(scalars, adjoint_mine, swap(adjoint_send), self_row, objectives, *totals)
    return (solution, adjoint)


def solution(mesh):
    in_specs = (
        P(("groups", "rows"), "cols"),
        P(("groups", "rows"), "cols"),
        P(("groups", "rows")),
        P(("groups", "cols")),
        P(("groups", "cols")),
        P(("groups", "rows")),
        P(None, "rows"),
        P(None, "rhs"),
        P("rhs"),
        P("rhs", "rows"),
    )
    out_specs = (P("rhs", ("groups", "rows", "cols")), P("rhs", ("groups", "rows", "cols")))
    return jax.shard_map(
        per_device, mesh=mesh, in_specs=in_specs, out_specs=out_specs, check_vma=False
    )
```

```python
import functools

import jax
import jax.numpy as jnp
from jax import lax
from jax.experimental import pallas as pl
from jax.experimental.pallas import tpu as pltpu
from jax.sharding import PartitionSpec as P

BLOCK = 8
LANES = 128
SHIFT = 3.0
GRID = ("rows", "cols", "rhs")
F32 = jnp.float32
BF16 = jnp.bfloat16

VMEM = pl.BlockSpec(memory_space=pltpu.VMEM)
SMEM = pl.BlockSpec(memory_space=pltpu.SMEM)
ANY = pl.BlockSpec(memory_space=pl.ANY)

CORE, COLUMNS, ROW, BEGIN, HOLDER, SPAN, CHUNKS = range(7)


def dot(left, right, dims):
    return lax.dot_general(left, right, (dims, ((), ())), preferred_element_type=F32)


def precise(left, right, dims):
    return lax.dot_general(
        left, right, (dims, ((), ())), precision=lax.Precision.HIGHEST, preferred_element_type=F32
    )


def low_onehot(index):
    low = jnp.bitwise_and(index, LANES - 1)
    hit = lax.broadcasted_iota(jnp.int32, (LANES, index.shape[1]), 0) == low
    return jnp.where(hit, 1.0, 0.0).astype(BF16)


def take_columns(field, index):
    rows, width = field.shape
    chunks = width // LANES
    stacked = jnp.concatenate(
        [field[:, i * LANES : (i + 1) * LANES] for i in range(chunks)], axis=0
    )
    picked = dot(stacked, low_onehot(index), ((1,), (0,)))
    high = jnp.right_shift(index, 7)
    total = jnp.zeros((rows, index.shape[1]), F32)
    for i in range(chunks):
        total = total + jnp.where(high == i, picked[i * rows : (i + 1) * rows], 0.0)
    return total


def put_columns(values, index, width):
    rows = values.shape[0]
    chunks = width // LANES
    high = jnp.right_shift(index, 7)
    stacked = jnp.concatenate(
        [jnp.where(high == i, values, 0.0).astype(BF16) for i in range(chunks)], axis=0
    )
    spread = dot(stacked, low_onehot(index), ((1,), (1,)))
    return jnp.concatenate([spread[i * rows : (i + 1) * rows] for i in range(chunks)], axis=1)


def both_cores(core, own, other):
    first = jnp.where(core == 0, own, other)
    second = jnp.where(core == 0, other, own)
    return jnp.concatenate([first, second], axis=0)


def right_kernel(
    half, scalars, pitch, pitch_other, modes, modes_other, blade, shapes, right, right_half
):
    core = scalars[CORE]
    blades = pitch.shape[0]
    blade_onehot = jnp.where(
        lax.broadcasted_iota(jnp.int32, (blades, blade.shape[1]), 0) == blade[...], 1.0, 0.0
    )
    for b in range(2):
        own = core == b
        amount = jnp.where(own, pitch[...], pitch_other[...])
        mode = jnp.where(own, modes[...], modes_other[...])
        mode_onehot = jnp.where(
            lax.broadcasted_iota(jnp.int32, (shapes.shape[0], BLOCK), 0) == mode, 1.0, 0.0
        )
        pattern = precise(mode_onehot, shapes[...], ((0,), (0,)))
        factor = precise(amount, blade_onehot, ((0,), (0,)))
        right[b * BLOCK : (b + 1) * BLOCK, :] = pattern * factor
    right_half[...] = right[:, pl.ds(pl.multiple_of(core * half, LANES), half)]


def local_wake(scalars, upper, lower):
    start = scalars[COLUMNS]
    return upper[...] - start, lower[...] - start


def load_adjoint_kernel(
    cuts, scalars, objectives, objectives_other, self_term, upper, lower, influence, wake,
    keep, give, start, target, self_half, held, whole, sems
):
    half = start.shape[1]
    piece = keep.shape[1]
    panels = 2 * piece
    core = scalars[CORE]
    first = core * half

    wake_copy = pltpu.make_async_copy(
        wake.at[pl.ds(pl.multiple_of(first, 16), half)],
        held.at[:, pl.ds(panels, wake.shape[1])],
        sems.at[len(cuts) - 1],
    )

    def panel_copy(i):
        begin, stop = cuts[i], cuts[i + 1]
        return pltpu.make_async_copy(
            influence.at[pl.ds(pl.multiple_of(first + begin, 16), stop - begin)],
            held.at[pl.ds(begin, stop - begin), pl.ds(0, panels)],
            sems.at[i],
        )

    wake_copy.start()
    for i in range(len(cuts) - 1):
        panel_copy(i).start()
    span = pl.ds(pl.multiple_of(first, LANES), half)
    target[...] = both_cores(core, objectives[:, span], objectives_other[:, span])
    self_half[...] = self_term[:, span]
    start[...] = target[...] / self_half[...]
    wake_copy.wait()
    carried = dot(start[...].astype(BF16), held[:, panels:], ((1,), (0,)))
    upper_local, lower_local = local_wake(scalars, upper, lower)
    whole[...] = put_columns(carried, upper_local, panels) - put_columns(
        carried, lower_local, panels
    )
    for i in range(len(cuts) - 1):
        panel_copy(i).wait()
        rows = slice(cuts[i], cuts[i + 1])
        whole[...] += dot(start[:, rows].astype(BF16), held[rows, 0:panels], ((1,), (0,)))
    keep[...] = whole[:, pl.ds(pl.multiple_of(core * piece, LANES), piece)]
    give[...] = whole[:, pl.ds(pl.multiple_of((1 - core) * piece, LANES), piece)]


def adjoint_piece(tile, scalars, field, which, carried, upper, lower, held, out):
    width = out.shape[1]
    piece = out.shape[0] // (2 * BLOCK) * width
    begin = which * piece
    upper_local, lower_local = local_wake(scalars, upper, lower)
    spread = put_columns(carried, upper_local - begin, piece) - put_columns(
        carried, lower_local - begin, piece
    )
    for start in range(0, piece, tile):
        span = pl.ds(pl.multiple_of(begin + start, LANES), tile)
        part = (
            dot(field, held[:, span], ((1,), (0,)))
            + spread[:, start : start + tile]
        )
        col, offset = divmod(start, width)
        for b in range(2):
            goal = (col * 2 + b) * BLOCK
            out[goal : goal + BLOCK, offset : offset + tile] = part[b * BLOCK : (b + 1) * BLOCK]


def adjoint_give_kernel(
    tile, n_in, scalars, previous, target, self_half, upper, lower, held, *rest
):
    parts, (give, adjoint, carried, mine, send) = rest[:n_in], rest[n_in:]
    image = self_half[...] * previous[...]
    for part in parts:
        image = image + part[...].astype(F32)
    adjoint[...] = previous[...] + (target[...] - image) / self_half[...]
    to_output(scalars, (adjoint,), mine, send)
    field = adjoint[...].astype(BF16)
    panels = held.shape[1] - carried.shape[1]
    carried[...] = dot(field, held[:, panels:], ((1,), (0,)))
    which = 1 - scalars[CORE]
    adjoint_piece(
        tile, scalars, field, which, carried[...], upper, lower, held, give
    )


def adjoint_keep_kernel(
    tile, scalars, adjoint, carried, upper, lower, held, ready, keep
):
    field = adjoint[...].astype(BF16)
    which = scalars[CORE]
    adjoint_piece(
        tile, scalars, field, which, carried[...], upper, lower, held, keep
    )


def forward_kernel(tile, places, split, scalars, upper, lower, held, *rest):
    shards, (out, field) = rest[: len(places)], rest[len(places) :]
    count = out.shape[0]
    for place, ref in zip(places, shards):
        span = pl.ds(pl.multiple_of(scalars[place], LANES), ref.shape[1])
        if split:
            high = ref[...].astype(BF16)
            field[0:count, span] = high
            field[count:, span] = (ref[...] - high.astype(F32)).astype(BF16)
        else:
            field[:, span] = ref[...]
    panels = held.shape[1] - upper.shape[1]
    source = field[:, 0:panels]
    upper_local, lower_local = local_wake(scalars, upper, lower)
    strength = take_columns(source, upper_local) - take_columns(source, lower_local)
    if split:
        strength = strength[0:count] + strength[count:]
        high = strength.astype(BF16)
        field[0:count, panels:] = high
        field[count:, panels:] = (strength - high.astype(F32)).astype(BF16)
    else:
        field[:, panels:] = strength.astype(BF16)
    for start in range(0, held.shape[0], tile):
        result = dot(field[...], held[start : start + tile, :], ((1,), (1,)))
        if split:
            result = result[0:count] + result[count:]
        out[:, start : start + tile] = result


def system_kernel(n_parts, scalars, basis, image, self_half, *rest):
    parts, (keep, give) = rest[:n_parts], rest[n_parts:]
    second = self_half[...] * image[...]
    for part in parts:
        second = second + part[...]
    first = image[...] + SHIFT * basis[...]
    core = scalars[CORE]
    keep[...] = jnp.zeros_like(keep)
    give[...] = jnp.zeros_like(give)
    for b in range(2):
        rows = slice(b * BLOCK, (b + 1) * BLOCK)
        images = jnp.concatenate([first[rows], second[rows]], axis=0)
        full = jnp.concatenate([images, basis[rows, :]], axis=0)
        system = precise(images, full, ((1,), (1,)))
        size = system.shape[1]

        @pl.when(core == b)
        def _():
            keep[:, 0:size] = system

        @pl.when(core != b)
        def _():
            give[:, 0:size] = system


def to_output(scalars, values, mine, send):
    width = mine.shape[1]
    core = scalars[CORE]
    span = pl.ds(pl.multiple_of(scalars[BEGIN], LANES), width)
    for i, value in enumerate(values):
        first = value[0:BLOCK, span]
        second = value[BLOCK : 2 * BLOCK, span]
        rows = slice(i * BLOCK, (i + 1) * BLOCK)
        mine[rows, :] = jnp.where(core == 0, first, second)
        send[rows, :] = jnp.where(core == 0, second, first)


def combine_kernel(scalars, keep, other, first, second):
    half = first.shape[1]
    low = (keep[:, 0:half] + other[:, 0:half]).astype(BF16)
    high = (keep[:, half:] + other[:, half:]).astype(BF16)
    odd = scalars[ROW] % 2 == 1
    first[...] = jnp.where(odd, high, low)
    second[...] = jnp.where(odd, low, high)


def image_kernel(n_parts, scalars, right_half, self_half, *rest):
    parts, (image, rounded, mine, send) = rest[:n_parts], rest[n_parts:]
    total = (self_half[...] - SHIFT) * right_half[...]
    for part in parts:
        total = total + part[...]
    image[...] = total
    rounded[...] = total.astype(BF16)
    to_output(scalars, (right_half, image), mine, send)


def collect_kernel(scalars, keep, other, *outs):
    for k, out in enumerate(outs):
        rows = pl.ds(pl.multiple_of(jnp.bitwise_xor(scalars[ROW], k) * BLOCK, BLOCK), BLOCK)
        out[...] = keep[rows, :] + other[rows, :]


def update_kernel(n_parts, scalars, mine, received, self_term, objectives, *rest):
    parts, out = rest[:n_parts], rest[n_parts]
    span = pl.ds(pl.multiple_of(scalars[SPAN], LANES), out.shape[1])
    previous = jnp.where(scalars[HOLDER] == 1, mine[...], received[...])
    scale = self_term[:, span]
    image = scale * previous
    for part in parts:
        image = image + part[...]
    out[...] = previous + (objectives[:, span] - image) / scale


def solve_kernel(n_parts, scalars, mine, received, *rest):
    parts, out = rest[:n_parts], rest[n_parts]
    basis = jnp.where(scalars[HOLDER] == 1, mine[...], received[...])
    system = parts[0][...]
    for part in parts[1:]:
        system = system + part[...]
    size = basis.shape[0]
    row = lax.broadcasted_iota(jnp.int32, (size, 1), 0)
    for j in range(size):
        pivot_row = system[j : j + 1, :] / system[j : j + 1, j : j + 1]
        factor = jnp.where(row == j, 0.0, system[:, j : j + 1])
        system = jnp.where(row == j, pivot_row, system - factor * pivot_row)
    weights = system[:, size : size + BLOCK]
    out[...] = precise(weights, basis, ((0,), (0,)))


def argument(value):
    return pltpu.with_memory_space_constraint(value, pltpu.HBM)


def keep_in_vmem(value):
    return pltpu.with_memory_space_constraint(value, pltpu.VMEM)


def params(mib=20):
    return pltpu.CompilerParams(vmem_limit_bytes=mib << 20)


def cost(flops, size):
    return pl.CostEstimate(flops=flops, bytes_accessed=size, transcendentals=0)


def per_device(
    influence,
    wake_influence,
    self_term,
    wake_upper,
    wake_lower,
    blade_of,
    mode_shapes,
    blade_pitch,
    design_map,
    objectives,
):
    influence = argument(influence)
    wake_influence = argument(wake_influence)
    n_rows, n_cols, n_rhs = (lax.axis_size(name) for name in GRID)
    side = n_cols * n_rhs
    piece, panels = influence.shape
    wake = wake_influence.shape[1]
    half = piece // n_rhs
    out_width = piece // n_cols
    count = 2 * BLOCK
    width = panels + wake
    if n_rows != side or n_rhs != 2 or panels != 2 * piece:
        raise ValueError("unsupported mesh")
    row_index = lax.axis_index("rows")
    col_index = lax.axis_index("cols")
    core = lax.axis_index("rhs")

    def cross(k):
        return [(a * side + b, b * side + (a ^ k)) for a in range(side) for b in range(side)]

    def fetch(j):
        return [
            (a * side + c * n_rhs + h, ((h ^ j) * n_cols + c) * side + a)
            for a in range(side)
            for c in range(n_cols)
            for h in range(n_rhs)
        ]

    def flip(k, size):
        return [(i, i ^ k) for i in range(size)]

    def swap(value):
        return lax.ppermute(value, "rhs", flip(1, 2))

    def cols_parts(value):
        return [value] + [lax.ppermute(value, "cols", flip(k, n_cols)) for k in range(1, n_cols)]

    near = core * piece
    far = (1 - core) * piece
    chunk_half = row_index // n_cols
    places = [
        near + chunk_half * half,
        near + (1 - chunk_half) * half,
        far + chunk_half * half,
        far + (1 - chunk_half) * half,
        near,
        far,
    ]
    span = col_index * out_width
    holder = (core == span // half).astype(jnp.int32)
    scalars = jnp.stack(
        [core, col_index * panels, row_index, span % half, holder, span] + places
    ).astype(jnp.int32)
    scalars = argument(scalars)
    self_row = argument(self_term[None, :])
    objectives = argument(objectives)
    upper = argument(wake_upper[None, :])
    lower = argument(wake_lower[None, :])

    cuts = [half * i // 8 for i in range(8)] + [half * 15 // 16, half]
    struct = jax.ShapeDtypeStruct

    modes = design_map[None, :]
    objectives_other = swap(objectives)
    right, right_half = pl.pallas_call(
        functools.partial(right_kernel, half),
        in_specs=[SMEM] + [VMEM] * 6,
        out_specs=[VMEM] * 2,
        out_shape=[struct((count, piece), F32), struct((count, half), F32)],
        compiler_params=params(4),
        name="right",
    )(
        scalars, argument(blade_pitch), (swap(blade_pitch)), argument(modes),
        (swap(modes)),
        argument(blade_of[None, :]), argument(mode_shapes),
    )
    right, objectives_other = lax.optimization_barrier((right, objectives_other))
    right_near = lax.ppermute(right, GRID, cross(0))

    keep, give, start, target, self_half, held = pl.pallas_call(
        functools.partial(load_adjoint_kernel, cuts),
        in_specs=[SMEM] + [VMEM] * 5 + [ANY, ANY],
        out_specs=[VMEM] * 6,
        out_shape=[
            struct((count, piece), F32),
            struct((count, piece), F32),
            struct((count, half), F32),
            struct((count, half), F32),
            struct((1, half), F32),
            pltpu.VMEM((half, width), BF16),
        ],
        scratch_shapes=[
            pltpu.VMEM((count, panels), F32),
            pltpu.SemaphoreType.DMA((len(cuts),)),
        ],
        compiler_params=params(),
        cost_estimate=cost(2 * count * half * width, 2 * half * width),
        name="adjoint_one",
    )(
        scalars, objectives, argument(objectives_other), self_row, upper, lower, influence, wake_influence
    )
    right_near, start = lax.optimization_barrier((right_near, start))
    right_far = swap(right_near)
    held = keep_in_vmem(held)

    def forward(places, shards, split, name):
        rows = 2 * count if split else count
        return pl.pallas_call(
            functools.partial(forward_kernel, 512, places, split),
            in_specs=[SMEM] + [VMEM] * (3 + len(shards)),
            out_specs=VMEM,
            out_shape=struct((count, half), F32),
            scratch_shapes=[pltpu.VMEM((rows, width), BF16)],
            compiler_params=params(),
            cost_estimate=cost(2 * count * half * width, 2 * half * width),
            name=name,
        )(scalars, upper, lower, held, *map(keep_in_vmem, shards))

    sends = pl.pallas_call(
        combine_kernel,
        in_specs=[SMEM] + [VMEM] * 2,
        out_specs=[VMEM] * 2,
        out_shape=[struct((count, half), BF16)] * 2,
        compiler_params=params(4),
        name="combine",
    )(scalars, argument(keep), swap(give))

    right_far, *sends = lax.optimization_barrier((right_far, *sends))
    induced = forward(
        (CHUNKS + 4, CHUNKS + 5), [right_near, right_far], True, "forward_one"
    )
    parts = [lax.ppermute(sends[k % 2], GRID, cross(k)) for k in range(side)]
    induced, *parts = lax.optimization_barrier((induced, *parts))

    tile = min(512, out_width)
    give, adjoint, carried, adjoint_mine, adjoint_send = pl.pallas_call(
        functools.partial(adjoint_give_kernel, tile, len(parts)),
        in_specs=[SMEM] + [VMEM] * (6 + len(parts)),
        out_specs=[VMEM] * 5,
        out_shape=[
            struct((side * BLOCK, out_width), F32),
            struct((count, half), F32),
            struct((count, wake), F32),
            struct((BLOCK, out_width), F32),
            struct((BLOCK, out_width), F32),
        ],
        compiler_params=params(),
        cost_estimate=cost(count * half * width, half * width),
        name="adjoint_two_give",
    )(
        scalars, start, target, self_half, upper, lower, held,
        *map(keep_in_vmem, parts),
    )
    induced = cols_parts(induced)
    give, *induced = lax.optimization_barrier((give, *induced))
    give = swap(give)
    image, image_rounded, bases_mine, bases_send = pl.pallas_call(
        functools.partial(image_kernel, len(induced)),
        in_specs=[SMEM] + [VMEM] * (2 + len(induced)),
        out_specs=[VMEM] * 4,
        out_shape=[
            struct((count, half), F32),
            struct((count, half), BF16),
            struct((count, out_width), F32),
            struct((count, out_width), F32),
        ],
        compiler_params=params(4),
        name="image",
    )(scalars, right_half, self_half, *induced)
    shards = [lax.ppermute(image_rounded, GRID, fetch(j)) for j in range(2)]
    keep = pl.pallas_call(
        functools.partial(adjoint_keep_kernel, tile),
        in_specs=[SMEM] + [VMEM] * 5 + [ANY],
        out_specs=VMEM,
        out_shape=struct((side * BLOCK, out_width), F32),
        compiler_params=params(),
        cost_estimate=cost(count * half * width, half * width),
        name="adjoint_two_keep",
    )(scalars, adjoint, carried, upper, lower, held, keep_in_vmem(image_rounded))

    keep, *shards = lax.optimization_barrier((keep, *shards))
    shards = shards + [swap(value) for value in shards]
    totals = pl.pallas_call(
        collect_kernel,
        in_specs=[SMEM, VMEM, VMEM],
        out_specs=[VMEM] * side,
        out_shape=[struct((BLOCK, out_width), F32)] * side,
        compiler_params=params(4),
        name="collect",
    )(scalars, argument(keep), give)
    bases_other, adjoint_other = swap(bases_send), swap(adjoint_send)
    *shards, first_total, bases_other, adjoint_other = lax.optimization_barrier(
        (*shards, totals[0], bases_other, adjoint_other)
    )
    totals = [first_total, *totals[1:]]
    induced = forward(tuple(CHUNKS + i for i in range(4)), shards, False, "forward_two")

    induced, *totals = lax.optimization_barrier((induced, *totals))
    totals = [lax.ppermute(totals[k], GRID, cross(k)) for k in range(side)]

    induced = cols_parts(induced)
    system_keep, system_give = pl.pallas_call(
        functools.partial(system_kernel, len(induced)),
        in_specs=[SMEM] + [VMEM] * (3 + len(induced)),
        out_specs=[VMEM] * 2,
        out_shape=[struct((count, LANES), F32)] * 2,
        compiler_params=params(4),
        name="system",
    )(scalars, right_half, image, self_half, *induced)
    system_other, *totals = lax.optimization_barrier((swap(system_give), *totals))
    system = system_keep + system_other
    systems = [system] + [lax.ppermute(system, "rows", flip(k, n_rows)) for k in range(1, n_rows)]
    solution = pl.pallas_call(
        functools.partial(solve_kernel, len(systems)),
        in_specs=[SMEM] + [VMEM] * (2 + len(systems)),
        out_specs=VMEM,
        out_shape=struct((BLOCK, out_width), F32),
        compiler_params=params(4),
        name="solve",
    )(scalars, bases_mine, bases_other, *systems)

    adjoint = pl.pallas_call(
        functools.partial(update_kernel, len(totals)),
        in_specs=[SMEM] + [VMEM] * (4 + len(totals)),
        out_specs=VMEM,
        out_shape=struct((BLOCK, out_width), F32),
        compiler_params=params(4),
        name="update",
    )(scalars, adjoint_mine, adjoint_other, self_row, objectives, *totals)
    return (solution, adjoint)


def solution(mesh):
    in_specs = (
        P(("groups", "rows"), "cols"),
        P(("groups", "rows"), "cols"),
        P(("groups", "rows")),
        P(("groups", "cols")),
        P(("groups", "cols")),
        P(("groups", "rows")),
        P(None, "rows"),
        P(None, "rhs"),
        P("rhs"),
        P("rhs", "rows"),
    )
    out_specs = (P("rhs", ("groups", "rows", "cols")), P("rhs", ("groups", "rows", "cols")))
    return jax.shard_map(
        per_device, mesh=mesh, in_specs=in_specs, out_specs=out_specs, check_vma=False
    )
```

```python
import functools

import jax
import jax.numpy as jnp
from jax import lax
from jax.experimental import pallas as pl
from jax.experimental.pallas import tpu as pltpu
from jax.sharding import PartitionSpec as P

BLOCK = 8
LANES = 128
SHIFT = 3.0
GRID = ("rows", "cols", "rhs")
F32 = jnp.float32
BF16 = jnp.bfloat16

VMEM = pl.BlockSpec(memory_space=pltpu.VMEM)
SMEM = pl.BlockSpec(memory_space=pltpu.SMEM)
ANY = pl.BlockSpec(memory_space=pl.ANY)

CORE, COLUMNS, ROW, BEGIN, HOLDER, SPAN, CHUNKS = range(7)


def dot(left, right, dims):
    return lax.dot_general(left, right, (dims, ((), ())), preferred_element_type=F32)


def precise(left, right, dims):
    return lax.dot_general(
        left, right, (dims, ((), ())), precision=lax.Precision.HIGHEST, preferred_element_type=F32
    )


def low_onehot(index):
    low = jnp.bitwise_and(index, LANES - 1)
    hit = lax.broadcasted_iota(jnp.int32, (LANES, index.shape[1]), 0) == low
    return jnp.where(hit, 1.0, 0.0).astype(BF16)


def take_columns(field, index):
    rows, width = field.shape
    chunks = width // LANES
    stacked = jnp.concatenate(
        [field[:, i * LANES : (i + 1) * LANES] for i in range(chunks)], axis=0
    )
    picked = dot(stacked, low_onehot(index), ((1,), (0,)))
    high = jnp.right_shift(index, 7)
    total = jnp.zeros((rows, index.shape[1]), F32)
    for i in range(chunks):
        total = total + jnp.where(high == i, picked[i * rows : (i + 1) * rows], 0.0)
    return total


def put_columns(values, index, width):
    rows = values.shape[0]
    chunks = width // LANES
    high = jnp.right_shift(index, 7)
    stacked = jnp.concatenate(
        [jnp.where(high == i, values, 0.0).astype(BF16) for i in range(chunks)], axis=0
    )
    spread = dot(stacked, low_onehot(index), ((1,), (1,)))
    return jnp.concatenate([spread[i * rows : (i + 1) * rows] for i in range(chunks)], axis=1)


def both_cores(core, own, other):
    first = jnp.where(core == 0, own, other)
    second = jnp.where(core == 0, other, own)
    return jnp.concatenate([first, second], axis=0)


def right_kernel(
    half, scalars, pitch, pitch_other, modes, modes_other, blade, shapes, right, right_half
):
    core = scalars[CORE]
    blades = pitch.shape[0]
    blade_onehot = jnp.where(
        lax.broadcasted_iota(jnp.int32, (blades, blade.shape[1]), 0) == blade[...], 1.0, 0.0
    )
    for b in range(2):
        own = core == b
        amount = jnp.where(own, pitch[...], pitch_other[...])
        mode = jnp.where(own, modes[...], modes_other[...])
        mode_onehot = jnp.where(
            lax.broadcasted_iota(jnp.int32, (shapes.shape[0], BLOCK), 0) == mode, 1.0, 0.0
        )
        pattern = precise(mode_onehot, shapes[...], ((0,), (0,)))
        factor = precise(amount, blade_onehot, ((0,), (0,)))
        right[b * BLOCK : (b + 1) * BLOCK, :] = pattern * factor
    right_half[...] = right[:, pl.ds(pl.multiple_of(core * half, LANES), half)]


def local_wake(scalars, upper, lower):
    start = scalars[COLUMNS]
    return upper[...] - start, lower[...] - start


def load_adjoint_kernel(
    cuts, scalars, objectives, objectives_other, self_term, upper, lower, influence, wake,
    keep, give, start, target, self_half, held, whole, sems
):
    half = start.shape[1]
    piece = keep.shape[1]
    panels = 2 * piece
    core = scalars[CORE]
    first = core * half

    wake_copy = pltpu.make_async_copy(
        wake.at[pl.ds(pl.multiple_of(first, 16), half)],
        held.at[:, pl.ds(panels, wake.shape[1])],
        sems.at[len(cuts) - 1],
    )

    def panel_copy(i):
        begin, stop = cuts[i], cuts[i + 1]
        return pltpu.make_async_copy(
            influence.at[pl.ds(pl.multiple_of(first + begin, 16), stop - begin)],
            held.at[pl.ds(begin, stop - begin), pl.ds(0, panels)],
            sems.at[i],
        )

    wake_copy.start()
    for i in range(len(cuts) - 1):
        panel_copy(i).start()
    span = pl.ds(pl.multiple_of(first, LANES), half)
    target[...] = both_cores(core, objectives[:, span], objectives_other[:, span])
    self_half[...] = self_term[:, span]
    start[...] = target[...] / self_half[...]
    wake_copy.wait()
    carried = dot(start[...].astype(BF16), held[:, panels:], ((1,), (0,)))
    upper_local, lower_local = local_wake(scalars, upper, lower)
    whole[...] = put_columns(carried, upper_local, panels) - put_columns(
        carried, lower_local, panels
    )
    for i in range(len(cuts) - 1):
        panel_copy(i).wait()
        rows = slice(cuts[i], cuts[i + 1])
        whole[...] += dot(start[:, rows].astype(BF16), held[rows, 0:panels], ((1,), (0,)))
    keep[...] = whole[:, pl.ds(pl.multiple_of(core * piece, LANES), piece)]
    give[...] = whole[:, pl.ds(pl.multiple_of((1 - core) * piece, LANES), piece)]


def adjoint_piece(tile, scalars, field, which, carried, upper, lower, held, out):
    width = out.shape[1]
    piece = out.shape[0] // (2 * BLOCK) * width
    begin = which * piece
    upper_local, lower_local = local_wake(scalars, upper, lower)
    spread = put_columns(carried, upper_local - begin, piece) - put_columns(
        carried, lower_local - begin, piece
    )
    for start in range(0, piece, tile):
        span = pl.ds(pl.multiple_of(begin + start, LANES), tile)
        part = (
            dot(field, held[:, span], ((1,), (0,)))
            + spread[:, start : start + tile]
        )
        col, offset = divmod(start, width)
        for b in range(2):
            goal = (col * 2 + b) * BLOCK
            out[goal : goal + BLOCK, offset : offset + tile] = part[b * BLOCK : (b + 1) * BLOCK]


def adjoint_give_kernel(
    tile, n_in, scalars, previous, target, self_half, upper, lower, held, *rest
):
    parts, (give, adjoint, carried, mine, send) = rest[:n_in], rest[n_in:]
    image = self_half[...] * previous[...]
    for part in parts:
        image = image + part[...].astype(F32)
    adjoint[...] = previous[...] + (target[...] - image) / self_half[...]
    to_output(scalars, (adjoint,), mine, send)
    field = adjoint[...].astype(BF16)
    panels = held.shape[1] - carried.shape[1]
    carried[...] = dot(field, held[:, panels:], ((1,), (0,)))
    which = 1 - scalars[CORE]
    adjoint_piece(
        tile, scalars, field, which, carried[...], upper, lower, held, give
    )


def adjoint_keep_kernel(
    tile, scalars, adjoint, carried, upper, lower, held, ready, keep
):
    field = adjoint[...].astype(BF16)
    which = scalars[CORE]
    adjoint_piece(
        tile, scalars, field, which, carried[...], upper, lower, held, keep
    )


def forward_kernel(tile, places, split, scalars, upper, lower, held, *rest):
    shards, (out, field) = rest[: len(places)], rest[len(places) :]
    count = out.shape[0]
    for place, ref in zip(places, shards):
        span = pl.ds(pl.multiple_of(scalars[place], LANES), ref.shape[1])
        if split:
            high = ref[...].astype(BF16)
            field[0:count, span] = high
            field[count:, span] = (ref[...] - high.astype(F32)).astype(BF16)
        else:
            field[:, span] = ref[...]
    panels = held.shape[1] - upper.shape[1]
    source = field[:, 0:panels]
    upper_local, lower_local = local_wake(scalars, upper, lower)
    strength = take_columns(source, upper_local) - take_columns(source, lower_local)
    if split:
        strength = strength[0:count] + strength[count:]
        high = strength.astype(BF16)
        field[0:count, panels:] = high
        field[count:, panels:] = (strength - high.astype(F32)).astype(BF16)
    else:
        field[:, panels:] = strength.astype(BF16)
    for start in range(0, held.shape[0], tile):
        result = dot(field[...], held[start : start + tile, :], ((1,), (1,)))
        if split:
            result = result[0:count] + result[count:]
        out[:, start : start + tile] = result


def system_kernel(n_parts, scalars, basis, image, self_half, *rest):
    parts, (keep, give) = rest[:n_parts], rest[n_parts:]
    second = self_half[...] * image[...]
    for part in parts:
        second = second + part[...]
    first = image[...] + SHIFT * basis[...]
    core = scalars[CORE]
    keep[...] = jnp.zeros_like(keep)
    give[...] = jnp.zeros_like(give)
    for b in range(2):
        rows = slice(b * BLOCK, (b + 1) * BLOCK)
        images = jnp.concatenate([first[rows], second[rows]], axis=0)
        full = jnp.concatenate([images, basis[rows, :]], axis=0)
        system = precise(images, full, ((1,), (1,)))
        size = system.shape[1]

        @pl.when(core == b)
        def _():
            keep[:, 0:size] = system

        @pl.when(core != b)
        def _():
            give[:, 0:size] = system


def to_output(scalars, values, mine, send):
    width = mine.shape[1]
    core = scalars[CORE]
    span = pl.ds(pl.multiple_of(scalars[BEGIN], LANES), width)
    for i, value in enumerate(values):
        first = value[0:BLOCK, span]
        second = value[BLOCK : 2 * BLOCK, span]
        rows = slice(i * BLOCK, (i + 1) * BLOCK)
        mine[rows, :] = jnp.where(core == 0, first, second)
        send[rows, :] = jnp.where(core == 0, second, first)


def combine_kernel(scalars, keep, other, first, second):
    half = first.shape[1]
    low = (keep[:, 0:half] + other[:, 0:half]).astype(BF16)
    high = (keep[:, half:] + other[:, half:]).astype(BF16)
    odd = scalars[ROW] % 2 == 1
    first[...] = jnp.where(odd, high, low)
    second[...] = jnp.where(odd, low, high)


def image_kernel(n_parts, scalars, right_half, self_half, *rest):
    parts, (image, rounded, mine, send) = rest[:n_parts], rest[n_parts:]
    total = (self_half[...] - SHIFT) * right_half[...]
    for part in parts:
        total = total + part[...]
    image[...] = total
    rounded[...] = total.astype(BF16)
    to_output(scalars, (right_half, image), mine, send)


def collect_kernel(scalars, keep, other, *outs):
    for k, out in enumerate(outs):
        rows = pl.ds(pl.multiple_of(jnp.bitwise_xor(scalars[ROW], k) * BLOCK, BLOCK), BLOCK)
        out[...] = (keep[rows, :] + other[rows, :]).astype(BF16)


def update_kernel(n_parts, scalars, mine, received, self_term, objectives, *rest):
    parts, out = rest[:n_parts], rest[n_parts]
    span = pl.ds(pl.multiple_of(scalars[SPAN], LANES), out.shape[1])
    previous = jnp.where(scalars[HOLDER] == 1, mine[...], received[...])
    scale = self_term[:, span]
    image = scale * previous
    for part in parts:
        image = image + part[...].astype(F32)
    out[...] = previous + (objectives[:, span] - image) / scale


def solve_kernel(n_parts, scalars, mine, received, *rest):
    parts, out = rest[:n_parts], rest[n_parts]
    basis = jnp.where(scalars[HOLDER] == 1, mine[...], received[...])
    system = parts[0][...]
    for part in parts[1:]:
        system = system + part[...]
    size = basis.shape[0]
    row = lax.broadcasted_iota(jnp.int32, (size, 1), 0)
    for j in range(size):
        pivot_row = system[j : j + 1, :] * (1.0 / system[j : j + 1, j : j + 1])
        factor = jnp.where(row == j, 0.0, system[:, j : j + 1])
        system = jnp.where(row == j, pivot_row, system - factor * pivot_row)
    weights = system[:, size : size + BLOCK]
    out[...] = precise(weights, basis, ((0,), (0,)))


def argument(value):
    return pltpu.with_memory_space_constraint(value, pltpu.HBM)


def keep_in_vmem(value):
    return pltpu.with_memory_space_constraint(value, pltpu.VMEM)


def params(mib=20):
    return pltpu.CompilerParams(vmem_limit_bytes=mib << 20)


def cost(flops, size):
    return pl.CostEstimate(flops=flops, bytes_accessed=size, transcendentals=0)


def per_device(
    influence,
    wake_influence,
    self_term,
    wake_upper,
    wake_lower,
    blade_of,
    mode_shapes,
    blade_pitch,
    design_map,
    objectives,
):
    influence = argument(influence)
    wake_influence = argument(wake_influence)
    n_rows, n_cols, n_rhs = (lax.axis_size(name) for name in GRID)
    side = n_cols * n_rhs
    piece, panels = influence.shape
    wake = wake_influence.shape[1]
    half = piece // n_rhs
    out_width = piece // n_cols
    count = 2 * BLOCK
    width = panels + wake
    if n_rows != side or n_rhs != 2 or panels != 2 * piece:
        raise ValueError("unsupported mesh")
    row_index = lax.axis_index("rows")
    col_index = lax.axis_index("cols")
    core = lax.axis_index("rhs")

    def cross(k):
        return [(a * side + b, b * side + (a ^ k)) for a in range(side) for b in range(side)]

    def fetch(j):
        return [
            (a * side + c * n_rhs + h, ((h ^ j) * n_cols + c) * side + a)
            for a in range(side)
            for c in range(n_cols)
            for h in range(n_rhs)
        ]

    def flip(k, size):
        return [(i, i ^ k) for i in range(size)]

    def swap(value):
        return lax.ppermute(value, "rhs", flip(1, 2))

    def cols_parts(value):
        return [value] + [lax.ppermute(value, "cols", flip(k, n_cols)) for k in range(1, n_cols)]

    near = core * piece
    far = (1 - core) * piece
    chunk_half = row_index // n_cols
    places = [
        near + chunk_half * half,
        near + (1 - chunk_half) * half,
        far + chunk_half * half,
        far + (1 - chunk_half) * half,
        near,
        far,
    ]
    span = col_index * out_width
    holder = (core == span // half).astype(jnp.int32)
    scalars = jnp.stack(
        [core, col_index * panels, row_index, span % half, holder, span] + places
    ).astype(jnp.int32)
    scalars = argument(scalars)
    self_row = argument(self_term[None, :])
    objectives = argument(objectives)
    upper = argument(wake_upper[None, :])
    lower = argument(wake_lower[None, :])

    cuts = [half * i // 8 for i in range(8)] + [half * 15 // 16, half]
    struct = jax.ShapeDtypeStruct

    modes = design_map[None, :]
    objectives_other = swap(objectives)
    right, right_half = pl.pallas_call(
        functools.partial(right_kernel, half),
        in_specs=[SMEM] + [VMEM] * 6,
        out_specs=[VMEM] * 2,
        out_shape=[struct((count, piece), F32), struct((count, half), F32)],
        compiler_params=params(4),
        name="right",
    )(
        scalars, argument(blade_pitch), (swap(blade_pitch)), argument(modes),
        (swap(modes)),
        argument(blade_of[None, :]), argument(mode_shapes),
    )
    right, objectives_other = lax.optimization_barrier((right, objectives_other))
    right_near = lax.ppermute(right, GRID, cross(0))

    keep, give, start, target, self_half, held = pl.pallas_call(
        functools.partial(load_adjoint_kernel, cuts),
        in_specs=[SMEM] + [VMEM] * 5 + [ANY, ANY],
        out_specs=[VMEM] * 6,
        out_shape=[
            struct((count, piece), F32),
            struct((count, piece), F32),
            struct((count, half), F32),
            struct((count, half), F32),
            struct((1, half), F32),
            pltpu.VMEM((half, width), BF16),
        ],
        scratch_shapes=[
            pltpu.VMEM((count, panels), F32),
            pltpu.SemaphoreType.DMA((len(cuts),)),
        ],
        compiler_params=params(),
        cost_estimate=cost(2 * count * half * width, 2 * half * width),
        name="adjoint_one",
    )(
        scalars, objectives, argument(objectives_other), self_row, upper, lower, influence, wake_influence
    )
    right_near, start = lax.optimization_barrier((right_near, start))
    right_far = swap(right_near)
    held = keep_in_vmem(held)

    def forward(places, shards, split, name):
        rows = 2 * count if split else count
        return pl.pallas_call(
            functools.partial(forward_kernel, 256, places, split),
            in_specs=[SMEM] + [VMEM] * (3 + len(shards)),
            out_specs=VMEM,
            out_shape=pltpu.VMEM((count, half), F32),
            scratch_shapes=[pltpu.VMEM((rows, width), BF16)],
            compiler_params=params(),
            cost_estimate=cost(2 * count * half * width, 2 * half * width),
            name=name,
        )(scalars, upper, lower, held, *map(keep_in_vmem, shards))

    sends = pl.pallas_call(
        combine_kernel,
        in_specs=[SMEM] + [VMEM] * 2,
        out_specs=[VMEM] * 2,
        out_shape=[struct((count, half), BF16)] * 2,
        compiler_params=params(4),
        name="combine",
    )(scalars, argument(keep), swap(give))

    right_far, *sends = lax.optimization_barrier((right_far, *sends))
    induced = forward(
        (CHUNKS + 4, CHUNKS + 5), [right_near, right_far], True, "forward_one"
    )
    parts = [lax.ppermute(sends[k % 2], GRID, cross(k)) for k in range(side)]
    induced, *parts = lax.optimization_barrier((induced, *parts))

    tile = min(512, out_width)
    give, adjoint, carried, adjoint_mine, adjoint_send = pl.pallas_call(
        functools.partial(adjoint_give_kernel, tile, len(parts)),
        in_specs=[SMEM] + [VMEM] * (6 + len(parts)),
        out_specs=[VMEM] * 5,
        out_shape=[
            pltpu.VMEM((side * BLOCK, out_width), F32),
            struct((count, half), F32),
            struct((count, wake), F32),
            struct((BLOCK, out_width), F32),
            struct((BLOCK, out_width), F32),
        ],
        compiler_params=params(),
        cost_estimate=cost(count * half * width, half * width),
        name="adjoint_two_give",
    )(
        scalars, start, target, self_half, upper, lower, held,
        *map(keep_in_vmem, parts),
    )
    induced = cols_parts(induced)
    give, *induced = lax.optimization_barrier((give, *induced))
    give = swap(give)
    image, image_rounded, bases_mine, bases_send = pl.pallas_call(
        functools.partial(image_kernel, len(induced)),
        in_specs=[SMEM] + [VMEM] * (2 + len(induced)),
        out_specs=[VMEM] * 4,
        out_shape=[
            struct((count, half), F32),
            struct((count, half), BF16),
            struct((count, out_width), F32),
            struct((count, out_width), F32),
        ],
        compiler_params=params(4),
        name="image",
    )(scalars, right_half, self_half, *induced)
    shards = [lax.ppermute(image_rounded, GRID, fetch(j)) for j in range(2)]
    keep = pl.pallas_call(
        functools.partial(adjoint_keep_kernel, tile),
        in_specs=[SMEM] + [VMEM] * 5 + [ANY],
        out_specs=VMEM,
        out_shape=pltpu.VMEM((side * BLOCK, out_width), F32),
        compiler_params=params(),
        cost_estimate=cost(count * half * width, half * width),
        name="adjoint_two_keep",
    )(scalars, adjoint, carried, upper, lower, held, keep_in_vmem(image_rounded))

    keep, *shards = lax.optimization_barrier((keep, *shards))
    shards = shards + [swap(value) for value in shards]
    totals = pl.pallas_call(
        collect_kernel,
        in_specs=[SMEM, VMEM, VMEM],
        out_specs=[VMEM] * side,
        out_shape=[struct((BLOCK, out_width), BF16)] * side,
        compiler_params=params(4),
        name="collect",
    )(scalars, keep, give)
    bases_other, adjoint_other = swap(bases_send), swap(adjoint_send)
    *shards, first_total, bases_other, adjoint_other = lax.optimization_barrier(
        (*shards, totals[0], bases_other, adjoint_other)
    )
    totals = [first_total, *totals[1:]]
    induced = forward(tuple(CHUNKS + i for i in range(4)), shards, False, "forward_two")

    induced, *totals = lax.optimization_barrier((induced, *totals))
    totals = [lax.ppermute(totals[k], GRID, cross(k)) for k in range(side)]

    induced = cols_parts(induced)
    system_keep, system_give = pl.pallas_call(
        functools.partial(system_kernel, len(induced)),
        in_specs=[SMEM] + [VMEM] * (3 + len(induced)),
        out_specs=[VMEM] * 2,
        out_shape=[struct((count, LANES), F32)] * 2,
        compiler_params=params(4),
        name="system",
    )(scalars, right_half, image, self_half, *induced)
    system_other, *totals = lax.optimization_barrier((swap(system_give), *totals))
    system = system_keep + system_other
    systems = [system] + [lax.ppermute(system, "rows", flip(k, n_rows)) for k in range(1, n_rows)]
    solution = pl.pallas_call(
        functools.partial(solve_kernel, len(systems)),
        in_specs=[SMEM] + [VMEM] * (2 + len(systems)),
        out_specs=VMEM,
        out_shape=struct((BLOCK, out_width), F32),
        compiler_params=params(4),
        name="solve",
    )(scalars, bases_mine, bases_other, *systems)

    adjoint = pl.pallas_call(
        functools.partial(update_kernel, len(totals)),
        in_specs=[SMEM] + [VMEM] * (4 + len(totals)),
        out_specs=VMEM,
        out_shape=struct((BLOCK, out_width), F32),
        compiler_params=params(4),
        name="update",
    )(scalars, adjoint_mine, adjoint_other, self_row, objectives, *totals)
    return (solution, adjoint)


def solution(mesh):
    in_specs = (
        P(("groups", "rows"), "cols"),
        P(("groups", "rows"), "cols"),
        P(("groups", "rows")),
        P(("groups", "cols")),
        P(("groups", "cols")),
        P(("groups", "rows")),
        P(None, "rows"),
        P(None, "rhs"),
        P("rhs"),
        P("rhs", "rows"),
    )
    out_specs = (P("rhs", ("groups", "rows", "cols")), P("rhs", ("groups", "rows", "cols")))
    return jax.shard_map(
        per_device, mesh=mesh, in_specs=in_specs, out_specs=out_specs, check_vma=False
    )
```

```python
import functools

import jax
import jax.numpy as jnp
from jax import lax
from jax.experimental import pallas as pl
from jax.experimental.pallas import tpu as pltpu
from jax.sharding import PartitionSpec as P

BLOCK = 8
LANES = 128
SHIFT = 3.0
GRID = ("rows", "cols", "rhs")
F32 = jnp.float32
BF16 = jnp.bfloat16

VMEM = pl.BlockSpec(memory_space=pltpu.VMEM)
SMEM = pl.BlockSpec(memory_space=pltpu.SMEM)
ANY = pl.BlockSpec(memory_space=pl.ANY)

CORE, COLUMNS, ROW, BEGIN, HOLDER, SPAN, CHUNKS = range(7)


def dot(left, right, dims):
    return lax.dot_general(left, right, (dims, ((), ())), preferred_element_type=F32)


def precise(left, right, dims):
    return lax.dot_general(
        left, right, (dims, ((), ())), precision=lax.Precision.HIGHEST, preferred_element_type=F32
    )


def low_onehot(index):
    low = jnp.bitwise_and(index, LANES - 1)
    hit = lax.broadcasted_iota(jnp.int32, (LANES, index.shape[1]), 0) == low
    return jnp.where(hit, 1.0, 0.0).astype(BF16)


def take_columns(field, index):
    rows, width = field.shape
    chunks = width // LANES
    stacked = jnp.concatenate(
        [field[:, i * LANES : (i + 1) * LANES] for i in range(chunks)], axis=0
    )
    picked = dot(stacked, low_onehot(index), ((1,), (0,)))
    high = jnp.right_shift(index, 7)
    total = jnp.zeros((rows, index.shape[1]), F32)
    for i in range(chunks):
        total = total + jnp.where(high == i, picked[i * rows : (i + 1) * rows], 0.0)
    return total


def put_columns(values, index, width):
    rows = values.shape[0]
    chunks = width // LANES
    high = jnp.right_shift(index, 7)
    stacked = jnp.concatenate(
        [jnp.where(high == i, values, 0.0).astype(BF16) for i in range(chunks)], axis=0
    )
    spread = dot(stacked, low_onehot(index), ((1,), (1,)))
    return jnp.concatenate([spread[i * rows : (i + 1) * rows] for i in range(chunks)], axis=1)


def both_cores(core, own, other):
    first = jnp.where(core == 0, own, other)
    second = jnp.where(core == 0, other, own)
    return jnp.concatenate([first, second], axis=0)


def right_kernel(
    half, scalars, pitch, pitch_other, modes, modes_other, blade, shapes, right, right_half
):
    core = scalars[CORE]
    blades = pitch.shape[0]
    blade_onehot = jnp.where(
        lax.broadcasted_iota(jnp.int32, (blades, blade.shape[1]), 0) == blade[...], 1.0, 0.0
    )
    for b in range(2):
        own = core == b
        amount = jnp.where(own, pitch[...], pitch_other[...])
        mode = jnp.where(own, modes[...], modes_other[...])
        mode_onehot = jnp.where(
            lax.broadcasted_iota(jnp.int32, (shapes.shape[0], BLOCK), 0) == mode, 1.0, 0.0
        )
        pattern = precise(mode_onehot, shapes[...], ((0,), (0,)))
        factor = precise(amount, blade_onehot, ((0,), (0,)))
        right[b * BLOCK : (b + 1) * BLOCK, :] = pattern * factor
    right_half[...] = right[:, pl.ds(pl.multiple_of(core * half, LANES), half)]


def local_wake(scalars, upper, lower):
    start = scalars[COLUMNS]
    return upper[...] - start, lower[...] - start


def load_adjoint_kernel(
    cuts, scalars, objectives, objectives_other, self_term, upper, lower, influence, wake,
    keep, give, start, target, self_half, held, whole, sems
):
    half = start.shape[1]
    piece = keep.shape[1]
    panels = 2 * piece
    core = scalars[CORE]
    first = core * half

    wake_copy = pltpu.make_async_copy(
        wake.at[pl.ds(pl.multiple_of(first, 16), half)],
        held.at[:, pl.ds(panels, wake.shape[1])],
        sems.at[len(cuts) - 1],
    )

    def panel_copy(i):
        begin, stop = cuts[i], cuts[i + 1]
        return pltpu.make_async_copy(
            influence.at[pl.ds(pl.multiple_of(first + begin, 16), stop - begin)],
            held.at[pl.ds(begin, stop - begin), pl.ds(0, panels)],
            sems.at[i],
        )

    wake_copy.start()
    for i in range(len(cuts) - 1):
        panel_copy(i).start()
    span = pl.ds(pl.multiple_of(first, LANES), half)
    target[...] = both_cores(core, objectives[:, span], objectives_other[:, span])
    self_half[...] = self_term[:, span]
    start[...] = target[...] / self_half[...]
    wake_copy.wait()
    carried = dot(start[...].astype(BF16), held[:, panels:], ((1,), (0,)))
    upper_local, lower_local = local_wake(scalars, upper, lower)
    whole[...] = put_columns(carried, upper_local, panels) - put_columns(
        carried, lower_local, panels
    )
    for i in range(len(cuts) - 1):
        panel_copy(i).wait()
        rows = slice(cuts[i], cuts[i + 1])
        whole[...] += dot(start[:, rows].astype(BF16), held[rows, 0:panels], ((1,), (0,)))
    keep[...] = whole[:, pl.ds(pl.multiple_of(core * piece, LANES), piece)]
    give[...] = whole[:, pl.ds(pl.multiple_of((1 - core) * piece, LANES), piece)]


def adjoint_piece(tile, scalars, field, which, carried, upper, lower, held, out):
    width = out.shape[1]
    piece = out.shape[0] // (2 * BLOCK) * width
    begin = which * piece
    upper_local, lower_local = local_wake(scalars, upper, lower)
    spread = put_columns(carried, upper_local - begin, piece) - put_columns(
        carried, lower_local - begin, piece
    )
    for start in range(0, piece, tile):
        span = pl.ds(pl.multiple_of(begin + start, LANES), tile)
        part = (
            dot(field, held[:, span], ((1,), (0,)))
            + spread[:, start : start + tile]
        )
        col, offset = divmod(start, width)
        for b in range(2):
            goal = (col * 2 + b) * BLOCK
            out[goal : goal + BLOCK, offset : offset + tile] = part[b * BLOCK : (b + 1) * BLOCK]


def adjoint_give_kernel(
    tile, n_in, scalars, previous, target, self_half, upper, lower, held, *rest
):
    parts, (give, adjoint, carried, mine, send) = rest[:n_in], rest[n_in:]
    image = self_half[...] * previous[...]
    for part in parts:
        image = image + part[...].astype(F32)
    adjoint[...] = previous[...] + (target[...] - image) / self_half[...]
    to_output(scalars, (adjoint,), mine, send)
    field = adjoint[...].astype(BF16)
    panels = held.shape[1] - carried.shape[1]
    carried[...] = dot(field, held[:, panels:], ((1,), (0,)))
    which = 1 - scalars[CORE]
    adjoint_piece(
        tile, scalars, field, which, carried[...], upper, lower, held, give
    )


def adjoint_keep_kernel(
    tile, scalars, adjoint, carried, upper, lower, held, ready, keep
):
    field = adjoint[...].astype(BF16)
    which = scalars[CORE]
    adjoint_piece(
        tile, scalars, field, which, carried[...], upper, lower, held, keep
    )


def forward_kernel(tile, places, split, scalars, upper, lower, held, *rest):
    shards, (out, field) = rest[: len(places)], rest[len(places) :]
    count = out.shape[0]
    for place, ref in zip(places, shards):
        span = pl.ds(pl.multiple_of(scalars[place], LANES), ref.shape[1])
        if split:
            high = ref[...].astype(BF16)
            field[0:count, span] = high
            field[count:, span] = (ref[...] - high.astype(F32)).astype(BF16)
        else:
            field[:, span] = ref[...]
    panels = held.shape[1] - upper.shape[1]
    source = field[:, 0:panels]
    upper_local, lower_local = local_wake(scalars, upper, lower)
    strength = take_columns(source, upper_local) - take_columns(source, lower_local)
    if split:
        strength = strength[0:count] + strength[count:]
        high = strength.astype(BF16)
        field[0:count, panels:] = high
        field[count:, panels:] = (strength - high.astype(F32)).astype(BF16)
    else:
        field[:, panels:] = strength.astype(BF16)
    for start in range(0, held.shape[0], tile):
        result = dot(field[...], held[start : start + tile, :], ((1,), (1,)))
        if split:
            result = result[0:count] + result[count:]
        out[:, start : start + tile] = result


def system_kernel(n_parts, scalars, basis, image, self_half, *rest):
    parts, (keep, give) = rest[:n_parts], rest[n_parts:]
    second = self_half[...] * image[...]
    for part in parts:
        second = second + part[...]
    first = image[...] + SHIFT * basis[...]
    core = scalars[CORE]
    keep[...] = jnp.zeros_like(keep)
    give[...] = jnp.zeros_like(give)
    for b in range(2):
        rows = slice(b * BLOCK, (b + 1) * BLOCK)
        images = jnp.concatenate([first[rows], second[rows]], axis=0)
        full = jnp.concatenate([images, basis[rows, :]], axis=0)
        system = precise(images, full, ((1,), (1,)))
        size = system.shape[1]

        @pl.when(core == b)
        def _():
            keep[:, 0:size] = system

        @pl.when(core != b)
        def _():
            give[:, 0:size] = system


def to_output(scalars, values, mine, send):
    width = mine.shape[1]
    core = scalars[CORE]
    span = pl.ds(pl.multiple_of(scalars[BEGIN], LANES), width)
    for i, value in enumerate(values):
        first = value[0:BLOCK, span]
        second = value[BLOCK : 2 * BLOCK, span]
        rows = slice(i * BLOCK, (i + 1) * BLOCK)
        mine[rows, :] = jnp.where(core == 0, first, second)
        send[rows, :] = jnp.where(core == 0, second, first)


def combine_kernel(scalars, keep, other, first, second):
    half = first.shape[1]
    low = (keep[:, 0:half] + other[:, 0:half]).astype(BF16)
    high = (keep[:, half:] + other[:, half:]).astype(BF16)
    odd = scalars[ROW] % 2 == 1
    first[...] = jnp.where(odd, high, low)
    second[...] = jnp.where(odd, low, high)


def image_kernel(n_parts, scalars, right_half, self_half, *rest):
    parts, (image, rounded, mine, send) = rest[:n_parts], rest[n_parts:]
    total = (self_half[...] - SHIFT) * right_half[...]
    for part in parts:
        total = total + part[...]
    image[...] = total
    rounded[...] = total.astype(BF16)
    to_output(scalars, (right_half, image), mine, send)


def collect_kernel(scalars, keep, other, *outs):
    for k, out in enumerate(outs):
        rows = pl.ds(pl.multiple_of(jnp.bitwise_xor(scalars[ROW], k) * BLOCK, BLOCK), BLOCK)
        out[...] = (keep[rows, :] + other[rows, :]).astype(BF16)


def update_kernel(n_parts, scalars, mine, received, self_term, objectives, *rest):
    parts, out = rest[:n_parts], rest[n_parts]
    span = pl.ds(pl.multiple_of(scalars[SPAN], LANES), out.shape[1])
    previous = jnp.where(scalars[HOLDER] == 1, mine[...], received[...])
    scale = self_term[:, span]
    image = scale * previous
    for part in parts:
        image = image + part[...].astype(F32)
    out[...] = previous + (objectives[:, span] - image) / scale


def solve_kernel(n_parts, scalars, mine, received, *rest):
    parts, out = rest[:n_parts], rest[n_parts]
    basis = jnp.where(scalars[HOLDER] == 1, mine[...], received[...])
    system = parts[0][...]
    for part in parts[1:]:
        system = system + part[...]
    size = basis.shape[0]
    row = lax.broadcasted_iota(jnp.int32, (size, 1), 0)
    for j in range(size):
        pivot_row = system[j : j + 1, :] * (1.0 / system[j : j + 1, j : j + 1])
        factor = jnp.where(row == j, 0.0, system[:, j : j + 1])
        system = jnp.where(row == j, pivot_row, system - factor * pivot_row)
    weights = system[:, size : size + BLOCK]
    out[...] = precise(weights, basis, ((0,), (0,)))


def argument(value):
    return pltpu.with_memory_space_constraint(value, pltpu.HBM)


def keep_in_vmem(value):
    return pltpu.with_memory_space_constraint(value, pltpu.VMEM)


def params(mib=20):
    return pltpu.CompilerParams(vmem_limit_bytes=mib << 20)


def cost(flops, size):
    return pl.CostEstimate(flops=flops, bytes_accessed=size, transcendentals=0)


def per_device(
    influence,
    wake_influence,
    self_term,
    wake_upper,
    wake_lower,
    blade_of,
    mode_shapes,
    blade_pitch,
    design_map,
    objectives,
):
    influence = argument(influence)
    wake_influence = argument(wake_influence)
    n_rows, n_cols, n_rhs = (lax.axis_size(name) for name in GRID)
    side = n_cols * n_rhs
    piece, panels = influence.shape
    wake = wake_influence.shape[1]
    half = piece // n_rhs
    out_width = piece // n_cols
    count = 2 * BLOCK
    width = panels + wake
    if n_rows != side or n_rhs != 2 or panels != 2 * piece:
        raise ValueError("unsupported mesh")
    row_index = lax.axis_index("rows")
    col_index = lax.axis_index("cols")
    core = lax.axis_index("rhs")

    def cross(k):
        return [(a * side + b, b * side + (a ^ k)) for a in range(side) for b in range(side)]

    def fetch(j):
        return [
            (a * side + c * n_rhs + h, ((h ^ j) * n_cols + c) * side + a)
            for a in range(side)
            for c in range(n_cols)
            for h in range(n_rhs)
        ]

    def flip(k, size):
        return [(i, i ^ k) for i in range(size)]

    def swap(value):
        return lax.ppermute(value, "rhs", flip(1, 2))

    def cols_parts(value):
        return [value] + [lax.ppermute(value, "cols", flip(k, n_cols)) for k in range(1, n_cols)]

    near = core * piece
    far = (1 - core) * piece
    chunk_half = row_index // n_cols
    places = [
        near + chunk_half * half,
        near + (1 - chunk_half) * half,
        far + chunk_half * half,
        far + (1 - chunk_half) * half,
        near,
        far,
    ]
    span = col_index * out_width
    holder = (core == span // half).astype(jnp.int32)
    scalars = jnp.stack(
        [core, col_index * panels, row_index, span % half, holder, span] + places
    ).astype(jnp.int32)
    scalars = argument(scalars)
    self_row = argument(self_term[None, :])
    objectives = argument(objectives)
    upper = argument(wake_upper[None, :])
    lower = argument(wake_lower[None, :])

    cuts = [half * i // 8 for i in range(8)] + [half * 15 // 16, half]
    struct = jax.ShapeDtypeStruct

    modes = design_map[None, :]
    objectives_other = swap(objectives)
    right, right_half = pl.pallas_call(
        functools.partial(right_kernel, half),
        in_specs=[SMEM] + [VMEM] * 6,
        out_specs=[VMEM] * 2,
        out_shape=[struct((count, piece), F32), struct((count, half), F32)],
        compiler_params=params(4),
        name="right",
    )(
        scalars, argument(blade_pitch), (swap(blade_pitch)), argument(modes),
        (swap(modes)),
        argument(blade_of[None, :]), argument(mode_shapes),
    )
    right, objectives_other = lax.optimization_barrier((right, objectives_other))
    right_near = lax.ppermute(right, GRID, cross(0))

    keep, give, start, target, self_half, held = pl.pallas_call(
        functools.partial(load_adjoint_kernel, cuts),
        in_specs=[SMEM] + [VMEM] * 5 + [ANY, ANY],
        out_specs=[VMEM] * 6,
        out_shape=[
            struct((count, piece), F32),
            struct((count, piece), F32),
            struct((count, half), F32),
            struct((count, half), F32),
            struct((1, half), F32),
            pltpu.VMEM((half, width), BF16),
        ],
        scratch_shapes=[
            pltpu.VMEM((count, panels), F32),
            pltpu.SemaphoreType.DMA((len(cuts),)),
        ],
        compiler_params=params(),
        cost_estimate=cost(2 * count * half * width, 2 * half * width),
        name="adjoint_one",
    )(
        scalars, objectives, argument(objectives_other), self_row, upper, lower, influence, wake_influence
    )
    right_near, start = lax.optimization_barrier((right_near, start))
    right_far = swap(right_near)
    held = keep_in_vmem(held)

    def forward(places, shards, split, name):
        rows = 2 * count if split else count
        return pl.pallas_call(
            functools.partial(forward_kernel, 256, places, split),
            in_specs=[SMEM] + [VMEM] * (3 + len(shards)),
            out_specs=VMEM,
            out_shape=pltpu.VMEM((count, half), F32),
            scratch_shapes=[pltpu.VMEM((rows, width), BF16)],
            compiler_params=params(),
            cost_estimate=cost(2 * count * half * width, 2 * half * width),
            name=name,
        )(scalars, upper, lower, held, *map(keep_in_vmem, shards))

    sends = pl.pallas_call(
        combine_kernel,
        in_specs=[SMEM] + [VMEM] * 2,
        out_specs=[VMEM] * 2,
        out_shape=[struct((count, half), BF16)] * 2,
        compiler_params=params(4),
        name="combine",
    )(scalars, argument(keep), swap(give))

    right_far, *sends = lax.optimization_barrier((right_far, *sends))
    induced = forward(
        (CHUNKS + 4, CHUNKS + 5), [right_near, right_far], True, "forward_one"
    )
    parts = [lax.ppermute(sends[k % 2], GRID, cross(k)) for k in range(side)]
    induced, *parts = lax.optimization_barrier((induced, *parts))

    tile = min(512, out_width)
    give, adjoint, carried, adjoint_mine, adjoint_send = pl.pallas_call(
        functools.partial(adjoint_give_kernel, tile, len(parts)),
        in_specs=[SMEM] + [VMEM] * (6 + len(parts)),
        out_specs=[VMEM] * 5,
        out_shape=[
            pltpu.VMEM((side * BLOCK, out_width), F32),
            struct((count, half), F32),
            struct((count, wake), F32),
            struct((BLOCK, out_width), F32),
            struct((BLOCK, out_width), F32),
        ],
        compiler_params=params(),
        cost_estimate=cost(count * half * width, half * width),
        name="adjoint_two_give",
    )(
        scalars, start, target, self_half, upper, lower, held,
        *map(keep_in_vmem, parts),
    )
    induced = cols_parts(induced)
    give, *induced = lax.optimization_barrier((give, *induced))
    give = swap(give)
    image, image_rounded, bases_mine, bases_send = pl.pallas_call(
        functools.partial(image_kernel, len(induced)),
        in_specs=[SMEM] + [VMEM] * (2 + len(induced)),
        out_specs=[VMEM] * 4,
        out_shape=[
            struct((count, half), F32),
            struct((count, half), BF16),
            struct((count, out_width), F32),
            struct((count, out_width), F32),
        ],
        compiler_params=params(4),
        name="image",
    )(scalars, right_half, self_half, *induced)
    shards = [lax.ppermute(image_rounded, GRID, fetch(j)) for j in range(2)]
    keep = pl.pallas_call(
        functools.partial(adjoint_keep_kernel, tile),
        in_specs=[SMEM] + [VMEM] * 5 + [ANY],
        out_specs=VMEM,
        out_shape=pltpu.VMEM((side * BLOCK, out_width), F32),
        compiler_params=params(),
        cost_estimate=cost(count * half * width, half * width),
        name="adjoint_two_keep",
    )(scalars, adjoint, carried, upper, lower, held, keep_in_vmem(image_rounded))

    keep, *shards = lax.optimization_barrier((keep, *shards))
    shards = shards + [swap(value) for value in shards]
    totals = pl.pallas_call(
        collect_kernel,
        in_specs=[SMEM, VMEM, VMEM],
        out_specs=[VMEM] * side,
        out_shape=[struct((BLOCK, out_width), BF16)] * side,
        compiler_params=params(4),
        name="collect",
    )(scalars, keep, give)
    *shards, first_total = lax.optimization_barrier((*shards, totals[0]))
    totals = [first_total, *totals[1:]]
    induced = forward(tuple(CHUNKS + i for i in range(4)), shards, False, "forward_two")

    induced, *totals = lax.optimization_barrier((induced, *totals))
    totals = [lax.ppermute(totals[k], GRID, cross(k)) for k in range(side)]

    induced = cols_parts(induced)
    system_keep, system_give = pl.pallas_call(
        functools.partial(system_kernel, len(induced)),
        in_specs=[SMEM] + [VMEM] * (3 + len(induced)),
        out_specs=[VMEM] * 2,
        out_shape=[struct((count, LANES), F32)] * 2,
        compiler_params=params(4),
        name="system",
    )(scalars, right_half, image, self_half, *induced)
    system_other, bases_send, adjoint_send, *totals = lax.optimization_barrier(
        (swap(system_give), bases_send, adjoint_send, *totals)
    )
    system = system_keep + system_other
    systems = [system] + [lax.ppermute(system, "rows", flip(k, n_rows)) for k in range(1, n_rows)]
    solution = pl.pallas_call(
        functools.partial(solve_kernel, len(systems)),
        in_specs=[SMEM] + [VMEM] * (2 + len(systems)),
        out_specs=VMEM,
        out_shape=struct((BLOCK, out_width), F32),
        compiler_params=params(4),
        name="solve",
    )(scalars, bases_mine, swap(bases_send), *systems)

    adjoint = pl.pallas_call(
        functools.partial(update_kernel, len(totals)),
        in_specs=[SMEM] + [VMEM] * (4 + len(totals)),
        out_specs=VMEM,
        out_shape=struct((BLOCK, out_width), F32),
        compiler_params=params(4),
        name="update",
    )(scalars, adjoint_mine, swap(adjoint_send), self_row, objectives, *totals)
    return (solution, adjoint)


def solution(mesh):
    in_specs = (
        P(("groups", "rows"), "cols"),
        P(("groups", "rows"), "cols"),
        P(("groups", "rows")),
        P(("groups", "cols")),
        P(("groups", "cols")),
        P(("groups", "rows")),
        P(None, "rows"),
        P(None, "rhs"),
        P("rhs"),
        P("rhs", "rows"),
    )
    out_specs = (P("rhs", ("groups", "rows", "cols")), P("rhs", ("groups", "rows", "cols")))
    return jax.shard_map(
        per_device, mesh=mesh, in_specs=in_specs, out_specs=out_specs, check_vma=False
    )
```
